256 devices in a mesh: ty: 8 (over x, z_lo), tx: 32 (over z_hi, y, core).
Axes of the slice: x: 4, y: 4, z: 8 (z_hi: 4, z_lo: 2; z = z_hi * 2 + z_lo), core: 2. Of those that a mesh axis runs over, the one named last changes fastest.
Arguments:
- mask_param: float32 [512, 4096], P('ty', 'tx'), may hold values from -12 to 12
- target: float32 [512, 4096], P('ty', 'tx'), may hold values from 0 to 1
- kernel_sets: bfloat16 [32, 8, 2, 128, 128], P('tx'), may hold values from -0.09375 to 0.09375
- kernel_weights: bfloat16 [32, 8], P('tx'), may hold values from 0.049804688 to 1
- tile_zones: int32 [8, 32, 2], P('ty', 'tx'), may hold values from 0 to 31
- tile_counts: int32 [8, 32], P('ty', 'tx'), may hold values from 1 to 2, as said below
- zone_to_set: int32 [32], replicated, may hold values from 0 to 31, each once
Outputs:
- resist: float32 [512, 4096], P('ty', 'tx')
- param_grad: float32 [512, 4096], P('ty', 'tx')
The draws below stay inside these ranges and needn't reach their ends.
Inputs may be any that keep to these rules, and one draw needn't show every extreme that they name: `tile_zones`: zone ids; a tile uses only its first tile_counts slots. `tile_counts`: some tile has 2 live slots. `zone_to_set`: each kernel set belongs to exactly one zone.
All inputs are finite; a program needn't handle non-finite values.
Results may differ from the reference program's by a relative error of at most 0.00045.
Values may be sent and summed in bfloat16 or wider, within the bound.
A program may use at most 128 MiB of HBM per device.

```python
import math
import jax
import jax.numpy as jnp
from jax import lax

TY_DEV = 64
TX_DEV = 128
K = 8
H = 64
ZSLOT = 2
KS = 128
NSET = 32
NZONE = 32
NY = 512
NX = 4096
FY = 192
FX = 384
N_TY = 8
N_TX = 32


def draw_tile_counts(key, part):
    key = jax.random.fold_in(key, 7)
    first, second, third = jax.random.split(key, 3)
    busy_tile = jax.random.randint(first, (N_TY, N_TX), 0, 4) == 0
    extra_count = jax.random.randint(second, (N_TY, N_TX), 2, ZSLOT + 1)
    counts = jnp.where(busy_tile, extra_count, 1).reshape(-1)
    chosen = jax.random.randint(third, (), 0, N_TY * N_TX)
    counts = counts.at[chosen].set(ZSLOT)
    return counts.reshape(N_TY, N_TX).astype(jnp.int32)


def with_ends(drawn, own_key, low, top_value):
    spot = [jax.random.randint(jax.random.fold_in(own_key, axis), (), 0, length) for axis, length in enumerate(drawn.shape)]
    main_axis = drawn.shape.index(max(drawn.shape))
    next_to = spot[:main_axis] + [(spot[main_axis] + 1) % drawn.shape[main_axis]] + spot[main_axis + 1:]
    return drawn.at[tuple(spot)].set(low).at[tuple(next_to)].set(top_value)


def shard_levels(rng, extent, shards, smallest, high):
    factor_of, own = 1.0, jax.random.fold_in(rng, 6)
    for axis_at, shards_of in shards:
        steps = jnp.exp(jax.random.uniform(jax.random.fold_in(own, axis_at), (shards_of,), jnp.float32, smallest / len(shards), high / len(shards)))
        factor_of = factor_of * jnp.repeat(steps, extent[axis_at] // shards_of).reshape([-1 if axis == axis_at else 1 for axis in range(len(extent))])
    return factor_of


def gaussian(rng, extent, deviation, most, shards=(), held_as=jnp.bfloat16):
    gain = shard_levels(rng, extent, shards, -0.22, 0.18) if shards else 1.0
    entries = jax.random.normal(rng, extent, jnp.float32) * deviation * gain
    return jnp.minimum(jnp.maximum(entries, -most), most).astype(held_as)


def setup_inputs(seed: int = 0) -> dict:
    arg_keys = jax.random.split(jax.random.key(seed), 8)
    return {
        "mask_param": gaussian(arg_keys[0], (NY, NX), 2.0, 12.0, ((0, 8), (1, 32)), jnp.float32),
        "target": jnp.clip(1.0 * jax.random.uniform(arg_keys[1], (NY, NX), jnp.float32) ** shard_levels(arg_keys[1], (NY, NX), ((0, 8), (1, 32)), -0.2, 0.2), 0.0, 1.0),
        "kernel_sets": gaussian(arg_keys[2], (NSET, K, 2, KS, KS), (0.75 / KS), 0.09375, ((0, 32),)),
        "kernel_weights": jnp.clip(jnp.exp(math.log(1.0) - 2.9996462 * jax.random.uniform(arg_keys[3], (NSET, K), jnp.float32) ** shard_levels(arg_keys[3], (NSET, K), ((0, 32),), -0.2, 0.2)), 0.049804688, 1.0).astype(jnp.bfloat16),
        "tile_zones": with_ends(jax.random.randint(arg_keys[4], (N_TY, N_TX, ZSLOT), 0, NZONE), jax.random.fold_in(arg_keys[4], 1), 0, NZONE - 1).astype(jnp.int32),
        "tile_counts": draw_tile_counts(jax.random.fold_in(arg_keys[7], 71), 0),
        "zone_to_set": jax.random.permutation(arg_keys[6], NSET).astype(jnp.int32),
    }


steepness = 8.0
threshold = 1.0
loss_weight = 16.0


def reference(mask_param, target, kernel_sets, kernel_weights, tile_zones, tile_counts, zone_to_set):
    mask_value = jax.nn.sigmoid(mask_param)
    padded = jnp.pad(mask_value, H)
    taps_all = kernel_sets.astype(jnp.float32)
    weights_all = kernel_weights.astype(jnp.float32)

    def one_tile(tile_index):
        tile_row = (tile_index // N_TX).astype(jnp.int32)
        tile_col = (tile_index % N_TX).astype(jnp.int32)
        extended = lax.dynamic_slice(padded, (tile_row * TY_DEV, tile_col * TX_DEV), (TY_DEV + 2 * H, TX_DEV + 2 * H))
        wanted = lax.dynamic_slice(target, (tile_row * TY_DEV, tile_col * TX_DEV), (TY_DEV, TX_DEV))
        set_index = zone_to_set[tile_zones[tile_row, tile_col]]
        count = tile_counts[tile_row, tile_col]
        blend = jnp.where(jnp.arange(ZSLOT) < count, 1.0 / count.astype(jnp.float32), 0.0).astype(jnp.float32)
        spectrum = jnp.fft.fft2(extended, s=(FY, FX))
        aerial = jnp.zeros((TY_DEV, TX_DEV), jnp.float32)
        fields = []
        for slot_index in range(ZSLOT):
            taps = taps_all[set_index[slot_index]]
            kernel = taps[:, 0] + 1j * taps[:, 1]
            backward = jnp.fft.ifft2(kernel, s=(FY, FX)) * (FY * FX)
            field_now = jnp.fft.ifft2(spectrum[None] * backward)[:, :TY_DEV, :TX_DEV]
            weights = weights_all[set_index[slot_index]]
            power = field_now.real ** 2 + field_now.imag ** 2
            aerial = aerial + blend[slot_index] * jnp.sum(weights[:, None, None] * power, axis=0)
            fields.append(field_now)
        resist = jax.nn.sigmoid(steepness * (aerial - threshold))
        slope = loss_weight * (resist - wanted) * steepness * resist * (1.0 - resist)
        total = jnp.zeros((FY, FX), spectrum.dtype)
        for slot_index in range(ZSLOT):
            taps = taps_all[set_index[slot_index]]
            kernel = taps[:, 0] + 1j * taps[:, 1]
            forward = jnp.fft.fft2(kernel, s=(FY, FX))
            weights = weights_all[set_index[slot_index]]
            source = 2.0 * slope[None] * blend[slot_index] * weights[:, None, None] * fields[slot_index]
            spread = jnp.fft.fft2(jnp.conj(source), s=(FY, FX))
            total = total + jnp.sum(spread * forward, axis=0)
        back_sum = jnp.fft.ifft2(total).real[:, :TX_DEV + 2 * H]
        return resist, back_sum

    resist_tiles, sums = lax.map(one_tile, jnp.arange(N_TY * N_TX, dtype=jnp.int32))
    resist = resist_tiles.reshape(N_TY, N_TX, TY_DEV, TX_DEV).transpose(0, 2, 1, 3).reshape(NY, NX)

    def place(tile_index, gather_sum):
        tile_row = (tile_index // N_TX).astype(jnp.int32)
        tile_col = (tile_index % N_TX).astype(jnp.int32)
        start = (tile_row * TY_DEV, tile_col * TX_DEV)
        piece = lax.dynamic_slice(gather_sum, start, (FY, TX_DEV + 2 * H)) + sums[tile_index]
        return lax.dynamic_update_slice(gather_sum, piece, start)

    initial = jnp.zeros((NY + 2 * H, NX + 2 * H), jnp.float32)
    summed = lax.fori_loop(0, N_TY * N_TX, place, initial)
    mask_grad = summed[H:H + NY, H:H + NX]
    param_grad = mask_grad * mask_value * (1.0 - mask_value)
    return resist, param_grad
```

```python
import functools

import jax
import jax.numpy as jnp
import ml_dtypes
import numpy as np
from jax import lax
from jax.experimental import pallas as pl
from jax.experimental.pallas import tpu as pltpu
from jax.sharding import PartitionSpec as P

BF = jnp.bfloat16
MESH = pl.DeviceIdType.MESH
XS, YC, ZH = 4, 8, 4
MEMBERS = XS * YC
TYS, TXS = 8, 32
AROUND = [(dr, dc) for dr in (-1, 0, 1) for dc in (-1, 0, 1) if (dr, dc) != (0, 0)]
E_ORDER = (4, 3, 5, 2, 6, 1, 7, 0)
DX_ORDER = (2, 1, 3, 0)


def tables():
    theta = np.pi * (2 * np.arange(128) + 1) / 256.0
    ky = 2 * np.pi / 192.0

    def split(a):
        hi = a.astype(ml_dtypes.bfloat16)
        lo = (a - hi.astype(np.float64)).astype(ml_dtypes.bfloat16)
        return hi, lo

    def left(a):
        hi, lo = split(a)
        return np.concatenate([hi, lo, hi], axis=1)

    def real_form(angle):
        c, s = np.cos(angle), np.sin(angle)
        return np.block([[c, -s], [s, c]])

    u, r, y = np.arange(192), np.arange(192), np.arange(64)
    ang = np.outer(np.arange(128), theta)
    hi, lo = split(np.concatenate([np.cos(ang), np.sin(ang)], axis=1))
    wk = np.concatenate([hi, lo], axis=0)
    a3 = left(real_form(ky * np.outer(u, np.arange(128))))
    b3 = left(real_form(ky * np.outer(y, u)))
    sc = 2.0 / (256 * 192)
    ang = np.outer(theta, np.arange(128))
    hi, lo = split(np.concatenate([np.cos(ang), -np.sin(ang)], axis=0) * sc)
    wi = np.concatenate([hi, lo], axis=1)
    ang = np.outer(np.arange(128), theta)
    hi, lo = split(np.concatenate([np.cos(ang), -np.sin(ang)], axis=1))
    wq = np.concatenate([hi, lo, hi], axis=0)
    aq3 = left(real_form(-ky * np.outer(u, y)))
    pos = np.arange(384) - 64
    live = ((pos >= 0) & (pos < 256)).astype(np.float64)
    ang = np.outer(pos, theta)
    hi, lo = split(np.concatenate([np.cos(ang), -np.sin(ang)], axis=1) * live[:, None])
    we = np.concatenate([hi, lo, hi], axis=0)
    ce3 = left(real_form(-ky * np.outer(u, r)))
    ct3 = left(real_form(ky * np.outer(r, u)))
    ang = np.outer(theta, pos)
    hi, lo = split(np.concatenate([np.cos(ang), -np.sin(ang)], axis=0) * sc * live[None, :])
    wt = np.concatenate([hi, lo, hi], axis=0)
    return dict(wk=wk, a3=a3, b3=b3, wi=wi, wq=wq, aq3=aq3, we=we, ce3=ce3, ct3=ct3, wt=wt)

NAMES = ("wk", "a3", "b3", "wi", "wq", "aq3", "we", "ce3", "ct3", "wt")

def hilo(a):
    hi = a.astype(BF)
    return hi, (a - hi.astype(jnp.float32)).astype(BF)

def dot(a, b):
    return jnp.dot(a, b, preferred_element_type=jnp.float32)

def rows3(a):
    hi, lo = hilo(a)
    return jnp.concatenate([hi, hi, lo], axis=0)

def cols3(a):
    hi, lo = hilo(a)
    return jnp.concatenate([hi, hi, lo], axis=1)

def swap(a):
    m, n = a.shape[0] // 2, a.shape[1] // 2
    top = jnp.concatenate([a[:m, :n], a[m:, :n]], axis=1)
    low = jnp.concatenate([a[:m, n:], a[m:, n:]], axis=1)
    return jnp.concatenate([top, low], axis=0)

def mask_spectrum(e9, we, ce3, e2):
    packed = dot(cols3(e9), we)
    tall = jnp.concatenate([packed[:, :128], packed[:, 128:]], axis=0)
    spec = dot(ce3, rows3(tall))
    e2[:, :128] = spec
    e2[:, 128:] = spec

def kernel_spectrum(tr, ti, t, k2, p):
    both = jnp.concatenate([tr, ti], axis=0)
    packed = dot(jnp.concatenate([both, both], axis=1), t["wk"][...])
    k2[p] = dot(t["a3"][...], rows3(swap(packed)))

def field(t, e2, k2, f, p):
    er, ei = e2[:192, :], e2[192:, :]
    kr, ki = k2[p, :192, :], k2[p, 192:, :]
    prod = jnp.concatenate([er * kr - ei * ki, er * ki + ei * kr], axis=0)
    z = swap(dot(t["b3"][...], rows3(prod)))
    hi, lo = hilo(z)
    first = dot(hi, t["wi"][...])
    out = first[:, :128] + first[:, 128:] + dot(lo, t["wi"][:, :128])
    f[p] = out
    return out

def spread(t, k2, q, p, tr, ti):
    packed = dot(cols3(q), t["wq"][...])
    q2 = dot(t["aq3"][...], rows3(swap(packed)))
    qr, qi = q2[:192], q2[192:]
    kr, ki = k2[p, :192, :], k2[p, 192:, :]
    tr[...] += qr * kr + qi * ki
    ti[...] += qi * kr - qr * ki

def back(t, tr, ti):
    total = jnp.concatenate([tr[:, :128] + tr[:, 128:], ti[:, :128] + ti[:, 128:]], axis=0)
    y = dot(t["ct3"][...], rows3(total))
    wide = jnp.concatenate([y[:192], y[192:]], axis=1)
    return dot(cols3(wide), t["wt"][...])

def slot_of(dr, dc):
    return (dr + 1) * 3 + dc + 1


def kernel(*refs):
    (mask_in, target_in, sets, wts, zones, counts, zone_to_set) = refs[:7]
    hbm = dict(zip(NAMES, refs[7:17]))
    resist_out, grad_out = refs[17:19]
    t = dict(zip(NAMES, refs[19:29]))
    (mask, target, value, tiles, chunks, info, sel, taps, wall, sv, wv, e2, k2, f, tr, ti, co, g9, gin,
     tab_sem, in_sem, own_sem, zsem, s_info, r_info, s_info2, r_info2, s_w, r_w, s_w2, r_w2,
     s1, r1, s2, r2, s_m, r_m, s_g, r_g) = refs[29:]

    ty, tx = lax.axis_index("ty"), lax.axis_index("tx")
    x, zl = ty // 2, ty % 2
    zh, yc = tx // YC, tx % YC
    me = x * YC + yc

    def remote(src, dst, send, recv, to):
        return pltpu.make_async_remote_copy(src, dst, send, recv, device_id=to, device_id_type=MESH)

    def done(ref, sem):
        pltpu.make_async_copy(ref, ref, sem).wait()

    copies_in = [pltpu.make_async_copy(mask_in, mask, in_sem.at[0]),
                 pltpu.make_async_copy(target_in, target, in_sem.at[1])]
    for c in copies_in:
        c.start()
    own = pltpu.make_async_copy(sets.at[me], chunks.at[tx], own_sem.at[0])
    own.start()
    tabs = [pltpu.make_async_copy(hbm[n], t[n], tab_sem.at[i]) for i, n in enumerate(NAMES)]
    for c in tabs:
        c.start()

    yc_line = [(yc + e) % YC for e in E_ORDER[:-1]]
    x_line = [(x + dx) % XS for dx in DX_ORDER[:-1]]
    up = 2 * zl + ZH - 1

    def z_target(m):
        if m == 3:
            return x * 2 + (1 - zl), (zh + 2) % ZH
        return x * 2 + (m - 1), (zh + up) % ZH

    z_sources = [(x * 2 + 1, (zh + ZH - 1) % ZH), (x * 2, (zh + 1) % ZH), (x * 2 + (1 - zl), (zh + 2) % ZH)]
    z_both = [(ty, (zh + ZH - 1) % ZH), (ty, (zh + 1) % ZH),
              (x * 2 + (1 - zl), (zh + up) % ZH), (x * 2 + (1 - zl), (zh + 2) % ZH)]

    def beside(dr, dc):
        return (ty + dr + TYS) % TYS, (tx + dc + TXS) % TXS

    bar = pltpu.get_barrier_semaphore()
    greet = [(a, b * YC + yc) for a, b in z_both]
    greet += [(a * 2 + zl, tx) for a in x_line]
    greet += [(ty, zh * YC + b) for b in yc_line]
    greet += [beside(dr, dc) for dr, dc in AROUND]
    for to in greet:
        pl.semaphore_signal(bar, 1, device_id=to, device_id_type=MESH)

    lane = lax.broadcasted_iota(jnp.int32, (1, 128), 1)
    my0, my1 = zone_to_set[zones[0]], zone_to_set[zones[1]]
    count = counts[0]
    sv[...] = jnp.where(lane == 0, my0, my1)
    wv[...] = jnp.concatenate([wts[...].astype(jnp.float32), jnp.zeros((1, 120), jnp.float32)], axis=1)
    for c in copies_in:
        c.wait()
    value[...] = 1.0 / (1.0 + jnp.exp(-mask[...]))

    pl.semaphore_wait(bar, len(greet))

    for i, a in enumerate(x_line):
        remote(sv, info.at[yc, x], s_info.at[i], r_info.at[i], (a * 2 + zl, tx)).start()
    for i, (a, b) in enumerate(z_sources):
        pl.semaphore_signal(zsem, 1, device_id=(a, b * YC + yc), device_id_type=MESH)
    for m in (3, 2, 1):
        a, b = z_target(m)
        remote(wv, wall.at[yc, zh], s_w, r_w, (a, b * YC + yc)).start()
    for m in (3, 2, 1):
        a, b = z_target(m)
        remote(sets.at[me], chunks.at[tx], s1, r1, (a, b * YC + yc)).start()
    for b in yc_line:
        remote(sets.at[x * YC + b], chunks.at[tx], s1, r1, (ty, zh * YC + b)).start()
    info[yc, x] = sv[...]
    wall[yc, zh] = wv[...]
    for i in range(3):
        done(info.at[0, 0], r_info.at[i])
    pl.semaphore_wait(zsem, 3)
    for m in (3, 2, 1):
        a, b = z_target(m)
        for y2 in yc_line:
            remote(sets.at[x * YC + y2], chunks.at[tx], s1, r1, (a, b * YC + y2)).start()
    for b in yc_line:
        remote(info.at[yc], info.at[yc], s_info2, r_info2, (ty, zh * YC + b)).start()
    done(wall.at[0, pl.ds(0, 3)], r_w)
    for b in yc_line:
        remote(wall.at[yc], wall.at[yc], s_w2, r_w2, (ty, zh * YC + b)).start()
    for dr, dc in AROUND:
        remote(value, tiles.at[slot_of(-dr, -dc)], s_m, r_m, beside(dr, dc)).start()
    tiles[slot_of(0, 0)] = value[...]
    for c in tabs:
        c.wait()
    done(tiles.at[pl.ds(0, 8)], r_m)

    def tile_at(dr, dc):
        block = tiles[slot_of(dr, dc)]
        if (dr, dc) == (0, 0):
            return block
        row, col = ty + dr, tx + dc
        inside = (row >= 0) & (row < TYS) & (col >= 0) & (col < TXS)
        return jnp.where(inside, block, 0.0)

    e9 = jnp.concatenate([jnp.concatenate([tile_at(dr, dc) for dc in (-1, 0, 1)], axis=1) for dr in (-1, 0, 1)], axis=0)
    mask_spectrum(e9, t["we"][...], t["ce3"][...], e2)
    own.wait()
    done(info.at[pl.ds(0, 7)], r_info2)
    done(chunks.at[pl.ds(0, 31)], r1)

    def select(i, s0, s1_):
        sel[i, 0] = chunks[s0]
        sel[i, 1] = chunks[s1_]

    for dx in DX_ORDER:
        for e in E_ORDER:
            if (dx, e) == (0, 0):
                continue
            x2, y2 = (x + dx) % XS, (yc + e) % YC
            row = info[y2, x2]
            i = dx * YC + e
            select(i, row[0, 0], row[0, 1])
            remote(sel.at[i], taps.at[me], s2, r2.at[dx], (x2 * 2 + zl, zh * YC + y2)).start()
    select(0, my0, my1)
    local = pltpu.make_async_copy(sel.at[0], taps.at[me], r2.at[0])
    local.start()

    for i in range(3):
        done(sv, s_info.at[i])
    done(wall.at[0, pl.ds(0, 3)], s_w)
    done(wall.at[pl.ds(0, 7)], r_w2)
    done(wall.at[pl.ds(0, 7)], s_w2)
    done(info.at[pl.ds(0, 7)], s_info2)
    done(tiles.at[pl.ds(0, 8)], s_m)
    done(chunks.at[pl.ds(0, 31)], s1)

    inverse = 1.0 / count.astype(jnp.float32)
    for j, s in enumerate((my0, my1)):
        row = wall[s % YC, s // YC]
        row = row * jnp.where(j < count, inverse, 0.0)
        for k in range(8):
            co[j * 8 + k] = jnp.broadcast_to(row[:, k:k + 1], (64, 128))

    aerial = jnp.zeros((64, 128), jnp.float32)
    for dx in DX_ORDER:
        done(taps.at[pl.ds(0, 8)], r2.at[dx])
        xs = (x + XS - dx) % XS

        def some(i, total):
            j, k = i // 2, 2 * xs + i % 2
            p = j * 8 + k
            first = jnp.concatenate([taps[4 * k, j], taps[4 * k + 1, j]], axis=0)
            second = jnp.concatenate([taps[4 * k + 2, j], taps[4 * k + 3, j]], axis=0)
            kernel_spectrum(first, second, t, k2, p)
            fp = field(t, e2, k2, f, p)
            return total + co[p] * (fp[:64] * fp[:64] + fp[64:] * fp[64:])

        aerial = lax.fori_loop(0, 4, some, aerial, unroll=2)

    done(sel.at[pl.ds(0, 31)], s2)
    resist = 1.0 / (1.0 + jnp.exp(-8.0 * (aerial - 1.0)))
    resist_out[...] = resist
    slope = 2.0 * (16.0 * (resist - target[...]) * 8.0 * resist * (1.0 - resist))
    tr[...] = jnp.zeros(tr.shape, jnp.float32)
    ti[...] = jnp.zeros(ti.shape, jnp.float32)

    def three(p, carry):
        g = slope * co[p]
        spread(t, k2, jnp.concatenate([g, g], axis=0) * f[p], p, tr, ti)
        return carry

    lax.fori_loop(0, 16, three, 0, unroll=2)
    g9[...] = back(t, tr, ti)
    for dr, dc in AROUND:
        src = g9.at[pl.ds((dr + 1) * 64, 64), pl.ds((dc + 1) * 128, 128)]
        remote(src, gin.at[slot_of(-dr, -dc)], s_g, r_g, beside(dr, dc)).start()
    gin[slot_of(0, 0)] = g9[64:128, 128:256]
    done(gin.at[pl.ds(0, 8)], r_g)
    total = gin[slot_of(0, 0)]
    for dr, dc in AROUND:
        row, col = ty + dr, tx + dc
        inside = (row >= 0) & (row < TYS) & (col >= 0) & (col < TXS)
        total = total + jnp.where(inside, gin[slot_of(dr, dc)], 0.0)
    m = value[...]
    grad_out[...] = total * m * (1.0 - m)
    done(gin.at[pl.ds(0, 8)], s_g)


def body(mask_param, target, kernel_sets, kernel_weights, tile_zones, tile_counts, zone_to_set):
    tb = tables()
    f32, i32, dma = jnp.float32, jnp.int32, pltpu.SemaphoreType.DMA
    any_, vmem = pl.BlockSpec(memory_space=pltpu.HBM), pl.BlockSpec(memory_space=pltpu.VMEM)
    smem = pl.BlockSpec(memory_space=pltpu.SMEM)
    scratch = [pltpu.VMEM(tb[n].shape, BF) for n in NAMES]
    scratch += [
        pltpu.VMEM((64, 128), f32), pltpu.VMEM((64, 128), f32), pltpu.VMEM((64, 128), f32),
        pltpu.VMEM((9, 64, 128), f32),
        pltpu.VMEM((32, 64, 128), BF), pltpu.VMEM((YC, XS, 1, 128), i32),
        pltpu.VMEM((32, 2, 64, 128), BF), pltpu.VMEM((32, 2, 64, 128), BF),
        pltpu.VMEM((YC, ZH, 1, 128), f32), pltpu.VMEM((1, 128), i32), pltpu.VMEM((1, 128), f32),
        pltpu.VMEM((384, 256), f32), pltpu.VMEM((16, 384, 256), f32), pltpu.VMEM((16, 128, 128), f32),
        pltpu.VMEM((192, 256), f32), pltpu.VMEM((192, 256), f32), pltpu.VMEM((16, 64, 128), f32),
        pltpu.VMEM((192, 384), f32), pltpu.VMEM((9, 64, 128), f32),
        dma((len(NAMES),)), dma((2,)), dma((1,)), pltpu.SemaphoreType.REGULAR,
        dma((3,)), dma((3,)), dma, dma, dma, dma, dma, dma,
        dma, dma, dma, dma((4,)), dma, dma, dma, dma,
    ]
    return pl.pallas_call(
        kernel,
        out_shape=(jax.ShapeDtypeStruct((64, 128), f32), jax.ShapeDtypeStruct((64, 128), f32)),
        in_specs=[any_, any_, any_, vmem, smem, smem, smem] + [any_] * len(NAMES),
        out_specs=(vmem, vmem),
        scratch_shapes=scratch,
        compiler_params=pltpu.CompilerParams(
            collective_id=1, has_side_effects=True, vmem_limit_bytes=63 << 20
        ),
        name="litho",
    )(
        mask_param, target, kernel_sets.reshape(32, 64, 128), kernel_weights,
        tile_zones.reshape(2), tile_counts.reshape(1), zone_to_set,
        *[jnp.asarray(tb[n]) for n in NAMES],
    )


def solution(mesh):
    in_specs = (
        P("ty", "tx"), P("ty", "tx"), P("tx", None, None, None, None), P("tx", None),
        P("ty", "tx", None), P("ty", "tx"), P(),
    )
    return jax.shard_map(
        body, mesh=mesh, in_specs=in_specs, out_specs=(P("ty", "tx"), P("ty", "tx")), check_vma=False
    )
```

```python
import functools

import jax
import jax.numpy as jnp
import ml_dtypes
import numpy as np
from jax import lax
from jax.experimental import pallas as pl
from jax.experimental.pallas import tpu as pltpu
from jax.sharding import PartitionSpec as P

BF = jnp.bfloat16
MESH = pl.DeviceIdType.MESH
XS, YC, ZH = 4, 8, 4
MEMBERS = XS * YC
TYS, TXS = 8, 32
AROUND = [(dr, dc) for dr in (-1, 0, 1) for dc in (-1, 0, 1) if (dr, dc) != (0, 0)]
E_ORDER = (4, 3, 5, 2, 6, 1, 7, 0)
DX_ORDER = (2, 1, 3, 0)
TY_ORDER = [(dx, dz) for dx in DX_ORDER for dz in (1, 0)]


def tables():
    theta = np.pi * (2 * np.arange(128) + 1) / 256.0
    ky = 2 * np.pi / 192.0

    def split(a):
        hi = a.astype(ml_dtypes.bfloat16)
        lo = (a - hi.astype(np.float64)).astype(ml_dtypes.bfloat16)
        return hi, lo

    def left(a):
        hi, lo = split(a)
        return np.concatenate([hi, lo, hi], axis=1)

    def real_form(angle):
        c, s = np.cos(angle), np.sin(angle)
        return np.block([[c, -s], [s, c]])

    u, r, y = np.arange(192), np.arange(192), np.arange(64)
    ang = np.outer(np.arange(128), theta)
    hi, lo = split(np.concatenate([np.cos(ang), np.sin(ang)], axis=1))
    wk = np.concatenate([hi, lo], axis=0)
    a3 = left(real_form(ky * np.outer(u, np.arange(128))))
    b3 = left(real_form(ky * np.outer(y, u)))
    sc = 2.0 / (256 * 192)
    ang = np.outer(theta, np.arange(128))
    hi, lo = split(np.concatenate([np.cos(ang), -np.sin(ang)], axis=0) * sc)
    wi = np.concatenate([hi, lo], axis=1)
    ang = np.outer(np.arange(128), theta)
    hi, lo = split(np.concatenate([np.cos(ang), -np.sin(ang)], axis=1))
    wq = np.concatenate([hi, lo, hi], axis=0)
    aq3 = left(real_form(-ky * np.outer(u, y)))
    pos = np.arange(384) - 64
    live = ((pos >= 0) & (pos < 256)).astype(np.float64)
    ang = np.outer(pos, theta)
    hi, lo = split(np.concatenate([np.cos(ang), -np.sin(ang)], axis=1) * live[:, None])
    we = np.concatenate([hi, lo, hi], axis=0)
    ce3 = left(real_form(-ky * np.outer(u, r)))
    ct3 = left(real_form(ky * np.outer(r, u)))
    ang = np.outer(theta, pos)
    hi, lo = split(np.concatenate([np.cos(ang), -np.sin(ang)], axis=0) * sc * live[None, :])
    wt = np.concatenate([hi, lo, hi], axis=0)
    return dict(wk=wk, a3=a3, b3=b3, wi=wi, wq=wq, aq3=aq3, we=we, ce3=ce3, ct3=ct3, wt=wt)

NAMES = ("wk", "a3", "b3", "wi", "wq", "aq3", "we", "ce3", "ct3", "wt")

def hilo(a):
    hi = a.astype(BF)
    return hi, (a - hi.astype(jnp.float32)).astype(BF)

def dot(a, b):
    return jnp.dot(a, b, preferred_element_type=jnp.float32)

def rows3(a):
    hi, lo = hilo(a)
    return jnp.concatenate([hi, hi, lo], axis=0)

def cols3(a):
    hi, lo = hilo(a)
    return jnp.concatenate([hi, hi, lo], axis=1)

def swap(a):
    m, n = a.shape[0] // 2, a.shape[1] // 2
    top = jnp.concatenate([a[:m, :n], a[m:, :n]], axis=1)
    low = jnp.concatenate([a[:m, n:], a[m:, n:]], axis=1)
    return jnp.concatenate([top, low], axis=0)

def mask_spectrum(e9, we, ce3, e2):
    packed = dot(cols3(e9), we)
    tall = jnp.concatenate([packed[:, :128], packed[:, 128:]], axis=0)
    spec = dot(ce3, rows3(tall))
    e2[:, :128] = spec
    e2[:, 128:] = spec

def kernel_spectrum(tr, ti, t, k2, p):
    both = jnp.concatenate([tr, ti], axis=0)
    packed = dot(jnp.concatenate([both, both], axis=1), t["wk"][...])
    k2[p] = dot(t["a3"][...], rows3(swap(packed)))

def field(t, e2, k2, f, p):
    er, ei = e2[:192, :], e2[192:, :]
    kr, ki = k2[p, :192, :], k2[p, 192:, :]
    prod = jnp.concatenate([er * kr - ei * ki, er * ki + ei * kr], axis=0)
    z = swap(dot(t["b3"][...], rows3(prod)))
    hi, lo = hilo(z)
    first = dot(hi, t["wi"][...])
    out = first[:, :128] + first[:, 128:] + dot(lo, t["wi"][:, :128])
    f[p] = out
    return out

def spread(t, k2, q, p, tr, ti):
    packed = dot(cols3(q), t["wq"][...])
    q2 = dot(t["aq3"][...], rows3(swap(packed)))
    qr, qi = q2[:192], q2[192:]
    kr, ki = k2[p, :192, :], k2[p, 192:, :]
    tr[...] += qr * kr + qi * ki
    ti[...] += qi * kr - qr * ki

def back(t, tr, ti):
    total = jnp.concatenate([tr[:, :128] + tr[:, 128:], ti[:, :128] + ti[:, 128:]], axis=0)
    y = dot(t["ct3"][...], rows3(total))
    wide = jnp.concatenate([y[:192], y[192:]], axis=1)
    return dot(cols3(wide), t["wt"][...])

def slot_of(dr, dc):
    return (dr + 1) * 3 + dc + 1


def kernel(*refs):
    (mask_in, target_in, sets, wts, zones, counts, zone_to_set) = refs[:7]
    hbm = dict(zip(NAMES, refs[7:17]))
    resist_out, grad_out = refs[17:19]
    t = dict(zip(NAMES, refs[19:29]))
    (mask, target, value, tiles, chunks, info, sel, taps, wall, sv, wv, e2, k2, f, tr, ti, co, g9, gin,
     tab_sem, in_sem, own_sem, zsem, s_info, r_info, s_info2, r_info2, s_w, r_w, s_w2, r_w2,
     s1, r1, s2, r2, s_m, r_m, s_g, r_g) = refs[29:]

    ty, tx = lax.axis_index("ty"), lax.axis_index("tx")
    x, zl = ty // 2, ty % 2
    zh, yc = tx // YC, tx % YC
    me = ty * YC + yc

    def remote(src, dst, send, recv, to):
        return pltpu.make_async_remote_copy(src, dst, send, recv, device_id=to, device_id_type=MESH)

    def done(ref, sem):
        pltpu.make_async_copy(ref, ref, sem).wait()

    copies_in = [pltpu.make_async_copy(mask_in, mask, in_sem.at[0]),
                 pltpu.make_async_copy(target_in, target, in_sem.at[1])]
    for c in copies_in:
        c.start()
    own = pltpu.make_async_copy(sets.at[me], chunks.at[tx], own_sem.at[0])
    own.start()
    tabs = [pltpu.make_async_copy(hbm[n], t[n], tab_sem.at[i]) for i, n in enumerate(NAMES)]
    for c in tabs:
        c.start()

    yc_line = [(yc + e) % YC for e in E_ORDER[:-1]]
    ty_line = [((x + dx) % XS) * 2 + (zl + dz) % 2 for dx, dz in TY_ORDER[:-1]]
    up = 2 * zl + ZH - 1

    def z_target(m):
        if m == 3:
            return x * 2 + (1 - zl), (zh + 2) % ZH
        return x * 2 + (m - 1), (zh + up) % ZH

    z_sources = [(x * 2 + 1, (zh + ZH - 1) % ZH), (x * 2, (zh + 1) % ZH), (x * 2 + (1 - zl), (zh + 2) % ZH)]
    z_both = [(ty, (zh + ZH - 1) % ZH), (ty, (zh + 1) % ZH),
              (x * 2 + (1 - zl), (zh + up) % ZH), (x * 2 + (1 - zl), (zh + 2) % ZH)]

    def beside(dr, dc):
        return (ty + dr + TYS) % TYS, (tx + dc + TXS) % TXS

    bar = pltpu.get_barrier_semaphore()
    greet = [(a, b * YC + yc) for a, b in z_both]
    greet += [(a, tx) for a in ty_line]
    greet += [(ty, zh * YC + b) for b in yc_line]
    greet += [beside(dr, dc) for dr, dc in AROUND]
    for to in greet:
        pl.semaphore_signal(bar, 1, device_id=to, device_id_type=MESH)

    lane = lax.broadcasted_iota(jnp.int32, (1, 128), 1)
    my0, my1 = zone_to_set[zones[0]], zone_to_set[zones[1]]
    count = counts[0]
    sv[...] = jnp.where(lane == 0, my0, my1)
    wv[...] = jnp.concatenate([wts[...].astype(jnp.float32), jnp.zeros((1, 120), jnp.float32)], axis=1)
    for c in copies_in:
        c.wait()
    value[...] = 1.0 / (1.0 + jnp.exp(-mask[...]))

    pl.semaphore_wait(bar, len(greet))

    for a in ty_line:
        remote(sv, info.at[yc, ty], s_info, r_info, (a, tx)).start()
    for i, (a, b) in enumerate(z_sources):
        pl.semaphore_signal(zsem, 1, device_id=(a, b * YC + yc), device_id_type=MESH)
    for m in (3, 2, 1):
        a, b = z_target(m)
        remote(wv, wall.at[yc, zh], s_w, r_w, (a, b * YC + yc)).start()
    for m in (3, 2, 1):
        a, b = z_target(m)
        remote(sets.at[a * YC + yc], chunks.at[tx], s1, r1, (a, b * YC + yc)).start()
    for b in yc_line:
        remote(sets.at[ty * YC + b], chunks.at[tx], s1, r1, (ty, zh * YC + b)).start()
    info[yc, ty] = sv[...]
    wall[yc, zh] = wv[...]
    done(info.at[0, pl.ds(0, 7)], r_info)
    pl.semaphore_wait(zsem, 3)
    for m in (3, 2, 1):
        a, b = z_target(m)
        for y2 in yc_line:
            remote(sets.at[a * YC + y2], chunks.at[tx], s1, r1, (a, b * YC + y2)).start()
    for b in yc_line:
        remote(info.at[yc], info.at[yc], s_info2, r_info2, (ty, zh * YC + b)).start()
    done(wall.at[0, pl.ds(0, 3)], r_w)
    for b in yc_line:
        remote(wall.at[yc], wall.at[yc], s_w2, r_w2, (ty, zh * YC + b)).start()
    for dr, dc in AROUND:
        remote(value, tiles.at[slot_of(-dr, -dc)], s_m, r_m, beside(dr, dc)).start()
    tiles[slot_of(0, 0)] = value[...]
    own.wait()
    done(info.at[pl.ds(0, 7)], r_info2)
    done(chunks.at[pl.ds(0, 31)], r1)


    def send_slot(j):
        for n, (dx, dz) in enumerate(TY_ORDER):
            ty2 = ((x + dx) % XS) * 2 + (zl + dz) % 2
            for e in E_ORDER:
                if (dx, dz, e) == (0, 0, 0):
                    continue
                y2 = (yc + e) % YC
                i = n * YC + e
                sel[j, i] = chunks[info[y2, ty2][0, j]]
                remote(sel.at[j, i], taps.at[j, me], s2.at[j], r2.at[j], (ty2, zh * YC + y2)).start()
        sel[j, 56] = chunks[(my0, my1)[j]]
        pltpu.make_async_copy(sel.at[j, 56], taps.at[j, me], r2.at[j]).start()

    send_slot(0)
    done(sel.at[0, pl.ds(0, 63)], s2.at[0])
    send_slot(1)

    for c in tabs:
        c.wait()
    done(tiles.at[pl.ds(0, 8)], r_m)

    def tile_at(dr, dc):
        block = tiles[slot_of(dr, dc)]
        if (dr, dc) == (0, 0):
            return block
        row, col = ty + dr, tx + dc
        inside = (row >= 0) & (row < TYS) & (col >= 0) & (col < TXS)
        return jnp.where(inside, block, 0.0)

    e9 = jnp.concatenate([jnp.concatenate([tile_at(dr, dc) for dc in (-1, 0, 1)], axis=1) for dr in (-1, 0, 1)], axis=0)
    mask_spectrum(e9, t["we"][...], t["ce3"][...], e2)
    done(info.at[0, pl.ds(0, 7)], s_info)
    done(wall.at[0, pl.ds(0, 3)], s_w)
    done(wall.at[pl.ds(0, 7)], r_w2)
    done(wall.at[pl.ds(0, 7)], s_w2)
    done(info.at[pl.ds(0, 7)], s_info2)
    done(tiles.at[pl.ds(0, 8)], s_m)
    done(chunks.at[pl.ds(0, 31)], s1)

    inverse = 1.0 / count.astype(jnp.float32)
    for j, s in enumerate((my0, my1)):
        row = wall[s % YC, s // YC]
        row = row * jnp.where(j < count, inverse, 0.0)
        for k in range(8):
            co[j * 8 + k] = jnp.broadcast_to(row[:, k:k + 1], (64, 128))

    aerial = jnp.zeros((64, 128), jnp.float32)
    for j in range(2):
        done(taps.at[j], r2.at[j])

        def spectra(k, carry):
            first, second = [taps[j, pl.ds(8 * k + 4 * i, 4)].reshape(128, 128) for i in range(2)]
            kernel_spectrum(first, second, t, k2, j * 8 + k)
            return carry

        def fields(k, total):
            p = j * 8 + k
            fp = field(t, e2, k2, f, p)
            return total + co[p] * (fp[:64] * fp[:64] + fp[64:] * fp[64:])

        lax.fori_loop(0, 8, spectra, 0, unroll=8)
        aerial = lax.fori_loop(0, 8, fields, aerial, unroll=8)

    done(sel.at[1, pl.ds(0, 63)], s2.at[1])
    resist = 1.0 / (1.0 + jnp.exp(-8.0 * (aerial - 1.0)))
    resist_out[...] = resist
    slope = 2.0 * (16.0 * (resist - target[...]) * 8.0 * resist * (1.0 - resist))
    tr[...] = jnp.zeros(tr.shape, jnp.float32)
    ti[...] = jnp.zeros(ti.shape, jnp.float32)

    def three(p, carry):
        g = slope * co[p]
        spread(t, k2, jnp.concatenate([g, g], axis=0) * f[p], p, tr, ti)
        return carry

    lax.fori_loop(0, 16, three, 0, unroll=8)
    g9[...] = back(t, tr, ti)
    for dr, dc in AROUND:
        src = g9.at[pl.ds((dr + 1) * 64, 64), pl.ds((dc + 1) * 128, 128)]
        remote(src, gin.at[slot_of(-dr, -dc)], s_g, r_g, beside(dr, dc)).start()
    gin[slot_of(0, 0)] = g9[64:128, 128:256]
    done(gin.at[pl.ds(0, 8)], r_g)
    total = gin[slot_of(0, 0)]
    for dr, dc in AROUND:
        row, col = ty + dr, tx + dc
        inside = (row >= 0) & (row < TYS) & (col >= 0) & (col < TXS)
        total = total + jnp.where(inside, gin[slot_of(dr, dc)], 0.0)
    m = value[...]
    grad_out[...] = total * m * (1.0 - m)
    done(gin.at[pl.ds(0, 8)], s_g)


def body(mask_param, target, kernel_sets, kernel_weights, tile_zones, tile_counts, zone_to_set):
    tb = tables()
    f32, i32, dma = jnp.float32, jnp.int32, pltpu.SemaphoreType.DMA
    any_, vmem = pl.BlockSpec(memory_space=pltpu.HBM), pl.BlockSpec(memory_space=pltpu.VMEM)
    smem = pl.BlockSpec(memory_space=pltpu.SMEM)
    scratch = [pltpu.VMEM(tb[n].shape, BF) for n in NAMES]
    scratch += [
        pltpu.VMEM((64, 128), f32), pltpu.VMEM((64, 128), f32), pltpu.VMEM((64, 128), f32),
        pltpu.VMEM((9, 64, 128), f32),
        pltpu.VMEM((32, 32, 128), BF), pltpu.VMEM((YC, TYS, 1, 128), i32),
        pltpu.VMEM((2, 64, 32, 128), BF), pltpu.VMEM((2, 64, 32, 128), BF),
        pltpu.VMEM((YC, ZH, 1, 128), f32), pltpu.VMEM((1, 128), i32), pltpu.VMEM((1, 128), f32),
        pltpu.VMEM((384, 256), f32), pltpu.VMEM((16, 384, 256), f32), pltpu.VMEM((16, 128, 128), f32),
        pltpu.VMEM((192, 256), f32), pltpu.VMEM((192, 256), f32), pltpu.VMEM((16, 64, 128), f32),
        pltpu.VMEM((192, 384), f32), pltpu.VMEM((9, 64, 128), f32),
        dma((len(NAMES),)), dma((2,)), dma((1,)), pltpu.SemaphoreType.REGULAR,
        dma, dma, dma, dma, dma, dma, dma, dma,
        dma, dma, dma((2,)), dma((2,)), dma, dma, dma, dma,
    ]
    return pl.pallas_call(
        kernel,
        out_shape=(jax.ShapeDtypeStruct((64, 128), f32), jax.ShapeDtypeStruct((64, 128), f32)),
        in_specs=[any_, any_, any_, vmem, smem, smem, smem] + [any_] * len(NAMES),
        out_specs=(vmem, vmem),
        scratch_shapes=scratch,
        compiler_params=pltpu.CompilerParams(
            collective_id=1, has_side_effects=True, vmem_limit_bytes=63 << 20
        ),
        name="litho",
    )(
        mask_param, target, kernel_sets.reshape(64, 32, 128), kernel_weights,
        tile_zones.reshape(2), tile_counts.reshape(1), zone_to_set,
        *[jnp.asarray(tb[n]) for n in NAMES],
    )


def solution(mesh):
    in_specs = (
        P("ty", "tx"), P("ty", "tx"), P("tx", None, None, None, None), P("tx", None),
        P("ty", "tx", None), P("ty", "tx"), P(),
    )
    return jax.shard_map(
        body, mesh=mesh, in_specs=in_specs, out_specs=(P("ty", "tx"), P("ty", "tx")), check_vma=False
    )
```

```python
import functools

import jax
import jax.numpy as jnp
import ml_dtypes
import numpy as np
from jax import lax
from jax.experimental import pallas as pl
from jax.experimental.pallas import tpu as pltpu
from jax.sharding import PartitionSpec as P

BF = jnp.bfloat16
MESH = pl.DeviceIdType.MESH
XS, YC, ZH = 4, 8, 4
MEMBERS = XS * YC
TYS, TXS = 8, 32
AROUND = [(dr, dc) for dr in (-1, 0, 1) for dc in (-1, 0, 1) if (dr, dc) != (0, 0)]
E_ORDER = (4, 3, 5, 2, 6, 1, 7, 0)
DX_ORDER = (2, 1, 3, 0)
TY_ORDER = [(dx, dz) for dx in DX_ORDER for dz in (1, 0)]


def tables():
    alpha = 2 * np.pi * (np.arange(96) + 0.5) / 192
    beta = 2 * np.pi * (np.arange(128) + 0.5) / 256
    scale = 2.0 / (192 * 256)

    def split(a):
        hi = a.astype(ml_dtypes.bfloat16)
        return hi, (a - hi.astype(np.float64)).astype(ml_dtypes.bfloat16)

    def left(a):
        hi, lo = split(a)
        return np.concatenate([hi, lo, hi], axis=1)

    def right(a):
        hi, lo = split(a)
        return np.concatenate([hi, lo, hi], axis=0)

    def down(n):
        ang = np.outer(alpha, np.arange(n))
        return np.concatenate([np.cos(ang), np.sin(ang)], axis=0)

    def across(pos):
        ang = np.outer(pos, beta)
        return np.concatenate([np.cos(ang), np.sin(ang)], axis=1)

    patch = np.concatenate([np.arange(64), np.arange(192, 256), np.arange(64, 192)])
    return dict(
        ky=np.concatenate(split(down(128)), axis=1),
        kx=right(across(np.arange(128))),
        fy=left(down(64).T),
        fx=np.concatenate(split(across(np.arange(128)).T * scale), axis=1),
        qy=left(down(64)),
        ex=right(across(patch)),
        ey=left(down(192)),
        gy=left(down(192).T),
        gx=right(across(patch).T * scale),
    )

NAMES = ("ky", "kx", "fy", "fx", "qy", "ex", "ey", "gy", "gx")

def hilo(a):
    hi = a.astype(BF)
    return hi, (a - hi.astype(jnp.float32)).astype(BF)

def dot(a, b):
    return jnp.dot(a, b, preferred_element_type=jnp.float32)

def rows3(a):
    hi, lo = hilo(a)
    return jnp.concatenate([hi, hi, lo], axis=0)

def cols3(a):
    hi, lo = hilo(a)
    return jnp.concatenate([hi, hi, lo], axis=1)

def pairs(z):
    cc, cs, sc, ss = z[:96, :128], z[:96, 128:], z[96:, :128], z[96:, 128:]
    re = jnp.concatenate([cc - ss, cc + ss], axis=1)
    im = jnp.concatenate([sc + cs, sc - cs], axis=1)
    return re, im

def unpair(re, im):
    p, r, q, s = re[:, :128], re[:, 128:], im[:, :128], im[:, 128:]
    top = jnp.concatenate([p + r, s - q], axis=1)
    low = jnp.concatenate([-(q + s), r - p], axis=1)
    return jnp.concatenate([top, low], axis=0)

def mask_spectrum(patch, t, e2):
    packed = dot(cols3(patch), t["ex"][...])
    re, im = pairs(dot(t["ey"][...], rows3(packed)))
    e2[:96] = re
    e2[96:] = -im

def kernel_spectrum(first, second, t, k2, p):
    wide = jnp.concatenate([first, second], axis=1)
    half = dot(t["ky"][...], jnp.concatenate([wide, wide], axis=0))
    tall = jnp.concatenate([half[:, :128], half[:, 128:]], axis=0)
    z = dot(cols3(tall), t["kx"][...])
    for i in range(2):
        re, im = pairs(z[192 * i:192 * i + 192])
        k2[p, i, :96] = re
        k2[p, i, 96:] = im

def field(t, e2, k2, f, p):
    er, ei = e2[:96], e2[96:]
    out = []
    for i in range(2):
        kr, ki = k2[p, i, :96], k2[p, i, 96:]
        out.append(dot(t["fy"][...], rows3(unpair(er * kr - ei * ki, er * ki + ei * kr))))
    hi, lo = hilo(jnp.concatenate(out, axis=0))
    first = dot(hi, t["fx"][...])
    res = first[:, :128] + first[:, 128:] + dot(lo, t["fx"][:, :128])
    f[p] = res
    return res

def spread(t, k2, q, p, tot):
    packed = dot(cols3(q), t["kx"][...])
    tr, ti = tot[:96], tot[96:]
    for i in range(2):
        qr, qi = pairs(dot(t["qy"][...], rows3(packed[64 * i:64 * i + 64])))
        kr, ki = k2[p, i, :96], k2[p, i, 96:]
        tr = tr + (qr * kr - qi * ki)
        ti = ti - (qi * kr + qr * ki)
    tot[:96] = tr
    tot[96:] = ti

def back(t, tot):
    y = dot(t["gy"][...], rows3(unpair(tot[:96], tot[96:])))
    return dot(cols3(y), t["gx"][...])

def pack(a):
    low = lax.broadcasted_iota(jnp.int32, (32, 128), 1) < 64
    top, bot = a[:32], a[32:]
    return jnp.where(low, top, pltpu.roll(bot, 64, 1)), jnp.where(low, pltpu.roll(top, 64, 1), bot)

def unpack(a, b):
    low = lax.broadcasted_iota(jnp.int32, (32, 128), 1) < 64
    return jnp.concatenate([jnp.where(low, a, pltpu.roll(b, 64, 1)), jnp.where(low, pltpu.roll(a, 64, 1), b)], axis=0)

def kernel(*refs):
    (mask_in, target_in, sets, wts, zones, counts, zone_to_set) = refs[:7]
    hbm = dict(zip(NAMES, refs[7:7 + len(NAMES)]))
    n = 7 + len(NAMES)
    resist_out, grad_out = refs[n:n + 2]
    t = dict(zip(NAMES, refs[n + 2:n + 2 + len(NAMES)]))
    (mask, target, value, halves, tall, side, chunks, info, sel, taps, wall, sv, wv, e2, k2, f, tot, co,
     gfull, ghalf, gtall, gside, want,
     tab_sem, in_sem, own_sem, s_info, r_info, s_info2, r_info2, s_w, r_w, s_w2, r_w2,
     s1, r1, s2, r2, s_m, r_m, s_m2, r_m2, s_g, r_g, s_g2, r_g2) = refs[n + 2 + len(NAMES):]

    ty, tx = lax.axis_index("ty"), lax.axis_index("tx")
    x, zl = ty // 2, ty % 2
    zh, yc = tx // YC, tx % YC
    me = ty * YC + yc

    def remote(src, dst, send, recv, to):
        return pltpu.make_async_remote_copy(src, dst, send, recv, device_id=to, device_id_type=MESH)

    def done(ref, sem):
        pltpu.make_async_copy(ref, ref, sem).wait()

    copies_in = [pltpu.make_async_copy(mask_in, mask, in_sem.at[0]),
                 pltpu.make_async_copy(target_in, target, in_sem.at[1])]
    for c in copies_in:
        c.start()
    own = pltpu.make_async_copy(sets.at[me], chunks.at[tx], own_sem.at[0])
    own.start()
    tabs = [pltpu.make_async_copy(hbm[n], t[n], tab_sem.at[i]) for i, n in enumerate(NAMES)]
    for c in tabs:
        c.start()

    yc_line = [(yc + e) % YC for e in E_ORDER[:-1]]
    ty_line = [((x + dx) % XS) * 2 + (zl + dz) % 2 for dx, dz in TY_ORDER[:-1]]
    up = 2 * zl + ZH - 1

    def z_target(m):
        if m == 3:
            return x * 2 + (1 - zl), (zh + 2) % ZH
        return x * 2 + (m - 1), (zh + up) % ZH

    z_sources = [(x * 2 + 1, (zh + ZH - 1) % ZH), (x * 2, (zh + 1) % ZH), (x * 2 + (1 - zl), (zh + 2) % ZH)]
    def beside(dr, dc):
        return (ty + dr + TYS) % TYS, (tx + dc + TXS) % TXS

    bar = pltpu.get_barrier_semaphore()
    greet = [(a, b * YC + (yc + e) % YC) for a, b in z_sources for e in E_ORDER]
    greet += [(a, tx) for a in ty_line]
    greet += [(ty, zh * YC + b) for b in yc_line]
    greet += [beside(dr, dc) for dr, dc in AROUND]
    for to in greet:
        pl.semaphore_signal(bar, 1, device_id=to, device_id_type=MESH)

    lane = lax.broadcasted_iota(jnp.int32, (1, 128), 1)
    my0, my1 = zone_to_set[zones[0]], zone_to_set[zones[1]]
    count = counts[0]
    sv[...] = jnp.where(lane == 0, my0, my1)
    wv[...] = jnp.concatenate([wts[...].astype(jnp.float32), jnp.zeros((1, 120), jnp.float32)], axis=1)
    for c in copies_in:
        c.wait()
    value[...] = 1.0 / (1.0 + jnp.exp(-mask[...]))
    halves[0], halves[1] = pack(value[...])

    pl.semaphore_wait(bar, len(greet))

    for a in ty_line:
        remote(sv, info.at[yc, ty], s_info, r_info, (a, tx)).start()
    for m in (3, 2, 1):
        a, b = z_target(m)
        remote(wv, wall.at[yc, zh], s_w, r_w, (a, b * YC + yc)).start()
    for m in (3, 2, 1):
        a, b = z_target(m)
        for e in E_ORDER:
            y2 = (yc + e) % YC
            remote(sets.at[a * YC + y2], chunks.at[tx], s1, r1, (a, b * YC + y2)).start()
    for b in yc_line:
        remote(sets.at[ty * YC + b], chunks.at[tx], s1, r1, (ty, zh * YC + b)).start()
    info[yc, ty] = sv[...]
    wall[yc, zh] = wv[...]
    done(info.at[0, pl.ds(0, 7)], r_info)
    for b in yc_line:
        remote(info.at[yc], info.at[yc], s_info2, r_info2, (ty, zh * YC + b)).start()
    done(wall.at[0, pl.ds(0, 3)], r_w)
    for b in yc_line:
        remote(wall.at[yc], wall.at[yc], s_w2, r_w2, (ty, zh * YC + b)).start()
    for dr in (-1, 0, 1):
        for dc in (-1, 1):
            remote(halves.at[(dc + 1) // 2], side.at[(1 - dr) * 2 + (1 - dc) // 2], s_m, r_m, beside(dr, dc)).start()
    for dr in (-1, 1):
        remote(value, tall.at[(1 - dr) // 2], s_m2, r_m2, beside(dr, 0)).start()
    own.wait()
    done(info.at[pl.ds(0, 7)], r_info2)
    to_scalars = pltpu.make_async_copy(info, want, own_sem.at[0])
    to_scalars.start()
    to_scalars.wait()
    done(chunks.at[pl.ds(0, 31)], r1)


    def send_slot(j):
        for n, (dx, dz) in enumerate(TY_ORDER):
            ty2 = ((x + dx) % XS) * 2 + (zl + dz) % 2
            for e in E_ORDER:
                if (dx, dz, e) == (0, 0, 0):
                    continue
                y2 = (yc + e) % YC
                i = n * YC + e
                sel[j, i] = chunks[want[y2, ty2, 0, j]]
                remote(sel.at[j, i], taps.at[j, me], s2.at[j], r2.at[j], (ty2, zh * YC + y2)).start()
        sel[j, 56] = chunks[(my0, my1)[j]]
        pltpu.make_async_copy(sel.at[j, 56], taps.at[j, me], r2.at[j]).start()

    send_slot(0)
    done(sel.at[0, pl.ds(0, 63)], s2.at[0])
    send_slot(1)

    for c in tabs:
        c.wait()
    done(side, r_m)
    done(tall, r_m2)

    def inside(dr, dc):
        row, col = ty + dr, tx + dc
        return (row >= 0) & (row < TYS) & (col >= 0) & (col < TXS)

    def gather(sides, talls, own_rows):
        blocks = []
        for dr in (-1, 0, 1):
            a, b = [jnp.where(inside(dr, dc), sides[(dr + 1) * 2 + (dc + 1) // 2], 0.0) for dc in (-1, 1)]
            mid = own_rows if dr == 0 else jnp.where(inside(dr, 0), talls[(dr + 1) // 2], 0.0)
            blocks.append((unpack(a, b), mid))
        return blocks

    blocks = gather(side, tall, value[...])
    mask_spectrum(jnp.concatenate([jnp.concatenate(b, axis=1) for b in blocks], axis=0), t, e2)
    done(info.at[0, pl.ds(0, 7)], s_info)
    done(wall.at[0, pl.ds(0, 3)], s_w)
    done(wall.at[pl.ds(0, 7)], r_w2)
    done(wall.at[pl.ds(0, 7)], s_w2)
    done(info.at[pl.ds(0, 7)], s_info2)
    done(side, s_m)
    done(tall, s_m2)
    done(chunks.at[pl.ds(0, 31)], s1)

    inverse = 1.0 / count.astype(jnp.float32)
    for j, s in enumerate((my0, my1)):
        row = wall[s % YC, s // YC]
        row = row * jnp.where(j < count, inverse, 0.0)
        for k in range(8):
            co[j * 8 + k] = jnp.broadcast_to(row[:, k:k + 1], (64, 128))

    aerial = jnp.zeros((64, 128), jnp.float32)
    for j in range(2):
        done(taps.at[j], r2.at[j])

        def spectra(k, carry):
            first, second = [taps[j, pl.ds(8 * k + 4 * i, 4)].reshape(128, 128) for i in range(2)]
            kernel_spectrum(first, second, t, k2, j * 8 + k)
            return carry

        def fields(k, total):
            p = j * 8 + k
            fp = field(t, e2, k2, f, p)
            return total + co[p] * (fp[:64] * fp[:64] + fp[64:] * fp[64:])

        lax.fori_loop(0, 8, spectra, 0, unroll=8)
        aerial = lax.fori_loop(0, 8, fields, aerial, unroll=8)

    done(sel.at[1, pl.ds(0, 63)], s2.at[1])
    resist = 1.0 / (1.0 + jnp.exp(-8.0 * (aerial - 1.0)))
    resist_out[...] = resist
    slope = 2.0 * (16.0 * (resist - target[...]) * 8.0 * resist * (1.0 - resist))
    tot[...] = jnp.zeros(tot.shape, jnp.float32)

    def three(p, carry):
        g = slope * co[p]
        spread(t, k2, jnp.concatenate([g, g], axis=0) * f[p], p, tot)
        return carry

    lax.fori_loop(0, 16, three, 0, unroll=8)
    g = back(t, tot)
    for dr in (-1, 1):
        gfull[(dr + 1) // 2] = g[(dr + 1) * 64:(dr + 2) * 64, 128:]
        remote(gfull.at[(dr + 1) // 2], gtall.at[(1 - dr) // 2], s_g2, r_g2, beside(dr, 0)).start()
    for dr in (-1, 0, 1):
        i = (dr + 1) * 2
        ghalf[i], ghalf[i + 1] = pack(g[(dr + 1) * 64:(dr + 2) * 64, :128])
        for dc in (-1, 1):
            remote(ghalf.at[i + (dc + 1) // 2], gside.at[(1 - dr) * 2 + (1 - dc) // 2], s_g, r_g, beside(dr, dc)).start()
    done(gtall, r_g2)
    done(gside, r_g)
    total = g[64:128, 128:]
    for from_sides, mid in gather(gside, gtall, 0.0):
        total = total + from_sides + mid
    m = value[...]
    grad_out[...] = total * m * (1.0 - m)
    done(gtall, s_g2)
    done(gside, s_g)


def body(mask_param, target, kernel_sets, kernel_weights, tile_zones, tile_counts, zone_to_set):
    tb = tables()
    f32, i32, dma = jnp.float32, jnp.int32, pltpu.SemaphoreType.DMA
    any_, vmem = pl.BlockSpec(memory_space=pltpu.HBM), pl.BlockSpec(memory_space=pltpu.VMEM)
    smem = pl.BlockSpec(memory_space=pltpu.SMEM)
    scratch = [pltpu.VMEM(tb[n].shape, BF) for n in NAMES]
    scratch += [
        pltpu.VMEM((64, 128), f32), pltpu.VMEM((64, 128), f32), pltpu.VMEM((64, 128), f32),
        pltpu.VMEM((2, 32, 128), f32), pltpu.VMEM((2, 64, 128), f32), pltpu.VMEM((6, 32, 128), f32),
        pltpu.VMEM((32, 32, 128), BF), pltpu.VMEM((YC, TYS, 1, 128), i32),
        pltpu.VMEM((2, 64, 32, 128), BF), pltpu.VMEM((2, 64, 32, 128), BF),
        pltpu.VMEM((YC, ZH, 1, 128), f32), pltpu.VMEM((1, 128), i32), pltpu.VMEM((1, 128), f32),
        pltpu.VMEM((192, 256), f32), pltpu.VMEM((16, 2, 192, 256), f32), pltpu.VMEM((16, 128, 128), f32),
        pltpu.VMEM((192, 256), f32), pltpu.VMEM((16, 64, 128), f32),
        pltpu.VMEM((2, 64, 128), f32), pltpu.VMEM((6, 32, 128), f32),
        pltpu.VMEM((2, 64, 128), f32), pltpu.VMEM((6, 32, 128), f32),
        pltpu.SMEM((YC, TYS, 1, 128), i32),
        dma((len(NAMES),)), dma((2,)), dma((1,)),
        dma, dma, dma, dma, dma, dma, dma, dma,
        dma, dma, dma((2,)), dma((2,)), dma, dma, dma, dma, dma, dma, dma, dma,
    ]
    return pl.pallas_call(
        kernel,
        out_shape=(jax.ShapeDtypeStruct((64, 128), f32), jax.ShapeDtypeStruct((64, 128), f32)),
        in_specs=[any_, any_, any_, vmem, smem, smem, smem] + [any_] * len(NAMES),
        out_specs=(vmem, vmem),
        scratch_shapes=scratch,
        compiler_params=pltpu.CompilerParams(
            collective_id=1, has_side_effects=True, vmem_limit_bytes=63 << 20
        ),
        name="litho",
    )(
        mask_param, target, kernel_sets.reshape(64, 32, 128), kernel_weights,
        tile_zones.reshape(2), tile_counts.reshape(1), zone_to_set,
        *[jnp.asarray(tb[n]) for n in NAMES],
    )


def solution(mesh):
    in_specs = (
        P("ty", "tx"), P("ty", "tx"), P("tx", None, None, None, None), P("tx", None),
        P("ty", "tx", None), P("ty", "tx"), P(),
    )
    return jax.shard_map(
        body, mesh=mesh, in_specs=in_specs, out_specs=(P("ty", "tx"), P("ty", "tx")), check_vma=False
    )
```

```python
import functools

import jax
import jax.numpy as jnp
import ml_dtypes
import numpy as np
from jax import lax
from jax.experimental import pallas as pl
from jax.experimental.pallas import tpu as pltpu
from jax.sharding import PartitionSpec as P

BF = jnp.bfloat16
GROUP = 4
MESH = pl.DeviceIdType.MESH
XS, YC, ZH = 4, 8, 4
TYS, TXS = 8, 32
AROUND = [(dr, dc) for dr in (-1, 0, 1) for dc in (-1, 0, 1) if (dr, dc) != (0, 0)]
E_ORDER = (4, 3, 5, 2, 6, 1, 7, 0)
DX_ORDER = (2, 1, 3, 0)
TY_ORDER = [(dx, dz) for dx in DX_ORDER for dz in (1, 0)]


def tables():
    alpha = 2 * np.pi * (np.arange(96) + 0.5) / 192
    beta = 2 * np.pi * (np.arange(128) + 0.5) / 256
    scale = 2.0 / (192 * 256)

    def split(a):
        hi = a.astype(ml_dtypes.bfloat16)
        return hi, (a - hi.astype(np.float64)).astype(ml_dtypes.bfloat16)

    def left(a):
        hi, lo = split(a)
        return np.concatenate([hi, lo, hi], axis=1)

    def right(a):
        hi, lo = split(a)
        return np.concatenate([hi, lo, hi], axis=0)

    def down(n):
        ang = np.outer(alpha, np.arange(n))
        return np.concatenate([np.cos(ang), np.sin(ang)], axis=0)

    def across(pos):
        ang = np.outer(pos, beta)
        return np.concatenate([np.cos(ang), np.sin(ang)], axis=1)

    patch = np.concatenate([np.arange(64), np.arange(192, 256), np.arange(64, 192)])
    return dict(
        ky=np.concatenate(split(down(128)), axis=1),
        kx=right(across(np.arange(128))),
        fy=left(down(64).T),
        fx=np.concatenate(split(across(np.arange(128)).T * scale), axis=1),
        qy=left(down(64)),
        ex=right(across(patch)),
        ey=left(down(192)),
        gy=left(down(192).T),
        gx=right(across(patch).T * scale),
    )

NAMES = ("ky", "kx", "fy", "fx", "qy", "ex", "ey", "gy", "gx")

def hilo(a):
    hi = a.astype(BF)
    return hi, (a - hi.astype(jnp.float32)).astype(BF)

def dot(a, b):
    return jnp.dot(a, b, preferred_element_type=jnp.float32)

def rows3(a):
    hi, lo = hilo(a)
    return jnp.concatenate([hi, hi, lo], axis=0)

def cols3(a):
    hi, lo = hilo(a)
    return jnp.concatenate([hi, hi, lo], axis=1)

def pairs(z):
    cc, cs, sc, ss = z[:96, :128], z[:96, 128:], z[96:, :128], z[96:, 128:]
    re = jnp.concatenate([cc - ss, cc + ss], axis=1)
    im = jnp.concatenate([sc + cs, sc - cs], axis=1)
    return re, im

def unpair(re, im):
    p, r, q, s = re[:, :128], re[:, 128:], im[:, :128], im[:, 128:]
    top = jnp.concatenate([p + r, s - q], axis=1)
    low = jnp.concatenate([-(q + s), r - p], axis=1)
    return jnp.concatenate([top, low], axis=0)

def mask_spectrum(patch, t, e2):
    packed = dot(cols3(patch), t["ex"][...])
    re, im = pairs(dot(t["ey"][...], rows3(packed)))
    e2[:96] = re
    e2[96:] = -im

def kernel_spectra(taps, t, k2, ps):
    wide = jnp.concatenate([c for pair in taps for c in pair], axis=1)
    half = dot(t["ky"][...], jnp.concatenate([wide, wide], axis=0))
    n = 2 * len(ps)
    tall = jnp.concatenate([half[:, 128 * i:128 * i + 128] for i in range(n)], axis=0)
    z = dot(cols3(tall), t["kx"][...])
    for i in range(n):
        re, im = pairs(z[192 * i:192 * i + 192])
        k2[ps[i // 2], i % 2, :96] = re
        k2[ps[i // 2], i % 2, 96:] = im


def fields_of(t, e2, k2, f, ps):
    er, ei = e2[:96], e2[96:]
    n = 2 * len(ps)
    parts = []
    for i in range(n):
        kr, ki = k2[ps[i // 2], i % 2, :96], k2[ps[i // 2], i % 2, 96:]
        parts.append(rows3(unpair(er * kr - ei * ki, er * ki + ei * kr)))
    y = dot(t["fy"][...], jnp.concatenate(parts, axis=1))
    hi, lo = hilo(jnp.concatenate([y[:, 256 * i:256 * i + 256] for i in range(n)], axis=0))
    first = dot(hi, t["fx"][...])
    res = first[:, :128] + first[:, 128:] + dot(lo, t["fx"][:, :128])
    for i, p in enumerate(ps):
        f[p] = res[128 * i:128 * i + 128]
    return [res[128 * i:128 * i + 128] for i in range(len(ps))]


def spread(t, k2, qs, ps, tot):
    packed = dot(cols3(jnp.concatenate(qs, axis=0)), t["kx"][...])
    for i in range(2 * len(ps)):
        qr, qi = pairs(dot(t["qy"][...], rows3(packed[64 * i:64 * i + 64])))
        kr, ki = k2[ps[i // 2], i % 2, :96], k2[ps[i // 2], i % 2, 96:]
        tot[:96] += qr * kr - qi * ki
        tot[96:] -= qi * kr + qr * ki


def back(t, tot):
    y = dot(t["gy"][...], rows3(unpair(tot[:96], tot[96:])))
    return dot(cols3(y), t["gx"][...])

def pack(a):
    low = lax.broadcasted_iota(jnp.int32, (32, 128), 1) < 64
    top, bot = a[:32], a[32:]
    return jnp.where(low, top, pltpu.roll(bot, 64, 1)), jnp.where(low, pltpu.roll(top, 64, 1), bot)

def unpack(a, b):
    low = lax.broadcasted_iota(jnp.int32, (32, 128), 1) < 64
    return jnp.concatenate([jnp.where(low, a, pltpu.roll(b, 64, 1)), jnp.where(low, pltpu.roll(a, 64, 1), b)], axis=0)

def kernel(*refs):
    (mask_in, target_in, sets, wts, zones, counts, zone_to_set) = refs[:7]
    hbm = dict(zip(NAMES, refs[7:7 + len(NAMES)]))
    n = 7 + len(NAMES)
    out = refs[n]
    t = dict(zip(NAMES, refs[n + 1:n + 1 + len(NAMES)]))
    (mask, target, value, halves, tall, side, chunks, info, sel, taps, wall, sv, wv, e2, k2, f, tot, co,
     gfull, ghalf, gtall, gside, want,
     tab_sem, in_sem, own_sem, s_info, r_info, s_info2, r_info2, s_w, r_w, s_w2, r_w2,
     s1, r1, s2, r2, s_m, r_m, s_m2, r_m2, s_g, r_g, s_g2, r_g2) = refs[n + 1 + len(NAMES):]

    ty, tx = lax.axis_index("ty"), lax.axis_index("tx")
    x, zl = ty // 2, ty % 2
    zh, yc = tx // YC, tx % YC
    me = ty * YC + yc

    def remote(src, dst, send, recv, to):
        return pltpu.make_async_remote_copy(src, dst, send, recv, device_id=to, device_id_type=MESH)

    def done(ref, sem):
        pltpu.make_async_copy(ref, ref, sem).wait()

    yc_line = [(yc + e) % YC for e in E_ORDER[:-1]]
    ty_line = [((x + dx) % XS) * 2 + (zl + dz) % 2 for dx, dz in TY_ORDER[:-1]]
    up = 2 * zl + ZH - 1

    def z_target(m):
        if m == 3:
            return x * 2 + (1 - zl), (zh + 2) % ZH
        return x * 2 + (m - 1), (zh + up) % ZH

    z_sources = [(x * 2 + 1, (zh + ZH - 1) % ZH), (x * 2, (zh + 1) % ZH), (x * 2 + (1 - zl), (zh + 2) % ZH)]
    def beside(dr, dc):
        return (ty + dr + TYS) % TYS, (tx + dc + TXS) % TXS

    bar = pltpu.get_barrier_semaphore()
    greet = [(a, b * YC + (yc + e) % YC) for a, b in z_sources for e in E_ORDER]
    greet += [(a, tx) for a in ty_line]
    greet += [(ty, zh * YC + b) for b in yc_line]
    greet += [beside(dr, dc) for dr, dc in AROUND if dc != 0]
    for to in greet:
        pl.semaphore_signal(bar, 1, device_id=to, device_id_type=MESH)

    copies_in = [pltpu.make_async_copy(mask_in, mask, in_sem.at[0]),
                 pltpu.make_async_copy(target_in, target, in_sem.at[1])]
    for c in copies_in:
        c.start()
    own = pltpu.make_async_copy(sets.at[me], chunks.at[tx], own_sem.at[0])
    own.start()
    tabs = [pltpu.make_async_copy(hbm[n], t[n], tab_sem.at[i]) for i, n in enumerate(NAMES)]
    for c in tabs:
        c.start()

    lane = lax.broadcasted_iota(jnp.int32, (1, 128), 1)
    my0, my1 = zone_to_set[zones[0]], zone_to_set[zones[1]]
    count = counts[0]
    sv[...] = jnp.where(lane == 0, my0, my1)
    wv[...] = jnp.concatenate([wts[...].astype(jnp.float32), jnp.zeros((1, 120), jnp.float32)], axis=1)
    for c in copies_in:
        c.wait()
    value[...] = 1.0 / (1.0 + jnp.exp(-mask[...]))
    halves[0], halves[1] = pack(value[...])

    pl.semaphore_wait(bar, len(greet))

    for a in ty_line:
        remote(sv, info.at[yc, ty], s_info, r_info, (a, tx)).start()
    for m in (3, 2, 1):
        a, b = z_target(m)
        remote(wv, wall.at[yc, zh], s_w, r_w, (a, b * YC + yc)).start()
    for m in (3, 2, 1):
        a, b = z_target(m)
        for e in E_ORDER:
            y2 = (yc + e) % YC
            remote(sets.at[a * YC + y2], chunks.at[tx], s1, r1, (a, b * YC + y2)).start()
    for b in yc_line:
        remote(sets.at[ty * YC + b], chunks.at[tx], s1, r1, (ty, zh * YC + b)).start()
    info[yc, ty] = sv[...]
    wall[yc, zh] = wv[...]
    done(info.at[0, pl.ds(0, 7)], r_info)
    for b in yc_line:
        remote(info.at[yc], info.at[yc], s_info2, r_info2, (ty, zh * YC + b)).start()
    done(wall.at[0, pl.ds(0, 3)], r_w)
    for b in yc_line:
        remote(wall.at[yc], wall.at[yc], s_w2, r_w2, (ty, zh * YC + b)).start()
    for dr in (-1, 0, 1):
        for dc in (-1, 1):
            remote(halves.at[(dc + 1) // 2], side.at[(1 - dr) * 2 + (1 - dc) // 2], s_m, r_m, beside(dr, dc)).start()
    for dr in (-1, 1):
        remote(value, tall.at[(1 - dr) // 2], s_m2, r_m2, beside(dr, 0)).start()
    own.wait()
    done(info.at[pl.ds(0, 7)], r_info2)
    to_scalars = pltpu.make_async_copy(info, want, own_sem.at[0])
    to_scalars.start()
    to_scalars.wait()
    done(chunks.at[pl.ds(0, 31)], r1)


    def send_slot(j):
        for n, (dx, dz) in enumerate(TY_ORDER):
            ty2 = ((x + dx) % XS) * 2 + (zl + dz) % 2
            for e in E_ORDER:
                if (dx, dz, e) == (0, 0, 0):
                    continue
                y2 = (yc + e) % YC
                i = n * YC + e
                sel[j, i] = chunks[want[y2, ty2, 0, j]]
                remote(sel.at[j, i], taps.at[j, me], s2.at[j], r2.at[j], (ty2, zh * YC + y2)).start()
        sel[j, 56] = chunks[(my0, my1)[j]]
        pltpu.make_async_copy(sel.at[j, 56], taps.at[j, me], r2.at[j]).start()

    send_slot(0)
    done(sel.at[0, pl.ds(0, 63)], s2.at[0])
    send_slot(1)

    for c in tabs:
        c.wait()
    done(side, r_m)
    done(tall, r_m2)

    def inside(dr, dc):
        row, col = ty + dr, tx + dc
        return (row >= 0) & (row < TYS) & (col >= 0) & (col < TXS)

    def gather(sides, talls, own_rows):
        blocks = []
        for dr in (-1, 0, 1):
            a, b = [jnp.where(inside(dr, dc), sides[(dr + 1) * 2 + (dc + 1) // 2], 0.0) for dc in (-1, 1)]
            mid = own_rows if dr == 0 else jnp.where(inside(dr, 0), talls[(dr + 1) // 2], 0.0)
            blocks.append((unpack(a, b), mid))
        return blocks

    blocks = gather(side, tall, value[...])
    mask_spectrum(jnp.concatenate([jnp.concatenate(b, axis=1) for b in blocks], axis=0), t, e2)
    done(info.at[0, pl.ds(0, 7)], s_info)
    done(wall.at[0, pl.ds(0, 3)], s_w)
    done(wall.at[pl.ds(0, 7)], r_w2)
    done(wall.at[pl.ds(0, 7)], s_w2)
    done(info.at[pl.ds(0, 7)], s_info2)
    done(side, s_m)
    done(tall, s_m2)
    done(chunks.at[pl.ds(0, 31)], s1)

    inverse = 1.0 / count.astype(jnp.float32)
    for j, s in enumerate((my0, my1)):
        row = wall[s % YC, s // YC]
        row = row * jnp.where(j < count, inverse, 0.0)
        for k in range(8):
            co[j * 8 + k] = jnp.broadcast_to(row[:, k:k + 1], (64, 128))

    aerial = jnp.zeros((64, 128), jnp.float32)
    for j in range(2):
        done(taps.at[j], r2.at[j])

        for h in range(0, 8, GROUP):
            chosen = [
                tuple(taps[j, 8 * k + 4 * i:8 * k + 4 * i + 4].reshape(128, 128) for i in range(2))
                for k in range(h, h + GROUP)
            ]
            kernel_spectra(chosen, t, k2, range(j * 8 + h, j * 8 + h + GROUP))
        for h in range(0, 8, GROUP):
            ps = range(j * 8 + h, j * 8 + h + GROUP)
            for p, fp in zip(ps, fields_of(t, e2, k2, f, ps)):
                aerial = aerial + co[p] * (fp[:64] * fp[:64] + fp[64:] * fp[64:])

    done(sel.at[1, pl.ds(0, 63)], s2.at[1])
    resist = 1.0 / (1.0 + jnp.exp(-8.0 * (aerial - 1.0)))
    out[0] = resist
    slope = 2.0 * (16.0 * (resist - target[...]) * 8.0 * resist * (1.0 - resist))
    tot[...] = jnp.zeros(tot.shape, jnp.float32)

    def some(h, carry):
        ps = [GROUP * h + i for i in range(GROUP)]
        spread(t, k2, [jnp.concatenate([slope * co[p]] * 2, axis=0) * f[p] for p in ps], ps, tot)
        return carry

    lax.fori_loop(0, 16 // GROUP, some, 0, unroll=2)
    g = back(t, tot)
    for dr in (-1, 1):
        gfull[(dr + 1) // 2] = g[(dr + 1) * 64:(dr + 2) * 64, 128:]
        remote(gfull.at[(dr + 1) // 2], gtall.at[(1 - dr) // 2], s_g2, r_g2, beside(dr, 0)).start()
    for dr in (-1, 0, 1):
        i = (dr + 1) * 2
        ghalf[i], ghalf[i + 1] = pack(g[(dr + 1) * 64:(dr + 2) * 64, :128])
        for dc in (-1, 1):
            remote(ghalf.at[i + (dc + 1) // 2], gside.at[(1 - dr) * 2 + (1 - dc) // 2], s_g, r_g, beside(dr, dc)).start()
    done(gtall, r_g2)
    done(gside, r_g)
    total = g[64:128, 128:]
    for from_sides, mid in gather(gside, gtall, 0.0):
        total = total + from_sides + mid
    m = value[...]
    out[1] = total * m * (1.0 - m)
    done(gtall, s_g2)
    done(gside, s_g)


def body(mask_param, target, kernel_sets, kernel_weights, tile_zones, tile_counts, zone_to_set):
    tb = tables()
    f32, i32, dma = jnp.float32, jnp.int32, pltpu.SemaphoreType.DMA
    any_, vmem = pl.BlockSpec(memory_space=pltpu.HBM), pl.BlockSpec(memory_space=pltpu.VMEM)
    smem = pl.BlockSpec(memory_space=pltpu.SMEM)
    scratch = [pltpu.VMEM(tb[n].shape, BF) for n in NAMES]
    scratch += [
        pltpu.VMEM((64, 128), f32), pltpu.VMEM((64, 128), f32), pltpu.VMEM((64, 128), f32),
        pltpu.VMEM((2, 32, 128), f32), pltpu.VMEM((2, 64, 128), f32), pltpu.VMEM((6, 32, 128), f32),
        pltpu.VMEM((32, 32, 128), BF), pltpu.VMEM((YC, TYS, 1, 128), i32),
        pltpu.VMEM((2, 64, 32, 128), BF), pltpu.VMEM((2, 64, 32, 128), BF),
        pltpu.VMEM((YC, ZH, 1, 128), f32), pltpu.VMEM((1, 128), i32), pltpu.VMEM((1, 128), f32),
        pltpu.VMEM((192, 256), f32), pltpu.VMEM((16, 2, 192, 256), f32), pltpu.VMEM((16, 128, 128), f32),
        pltpu.VMEM((192, 256), f32), pltpu.VMEM((16, 64, 128), f32),
        pltpu.VMEM((2, 64, 128), f32), pltpu.VMEM((6, 32, 128), f32),
        pltpu.VMEM((2, 64, 128), f32), pltpu.VMEM((6, 32, 128), f32),
        pltpu.SMEM((YC, TYS, 1, 128), i32),
        dma((len(NAMES),)), dma((2,)), dma((1,)),
        dma, dma, dma, dma, dma, dma, dma, dma,
        dma, dma, dma((2,)), dma((2,)), dma, dma, dma, dma, dma, dma, dma, dma,
    ]
    out = pl.pallas_call(
        kernel,
        out_shape=jax.ShapeDtypeStruct((2, 64, 128), f32),
        in_specs=[any_, any_, any_, vmem, smem, smem, smem] + [any_] * len(NAMES),
        out_specs=vmem,
        scratch_shapes=scratch,
        compiler_params=pltpu.CompilerParams(
            collective_id=1, has_side_effects=True, vmem_limit_bytes=63 << 20
        ),
        name="litho",
    )(
        mask_param, target, kernel_sets.reshape(64, 32, 128), kernel_weights,
        tile_zones.reshape(2), tile_counts.reshape(1), zone_to_set,
        *[jnp.asarray(tb[n]) for n in NAMES],
    )
    return out[0], out[1]


def solution(mesh):
    in_specs = (
        P("ty", "tx"), P("ty", "tx"), P("tx", None, None, None, None), P("tx", None),
        P("ty", "tx", None), P("ty", "tx"), P(),
    )
    return jax.shard_map(
        body, mesh=mesh, in_specs=in_specs, out_specs=(P("ty", "tx"), P("ty", "tx")), check_vma=False
    )
```

```python
import functools

import jax
import jax.numpy as jnp
import ml_dtypes
import numpy as np
from jax import lax
from jax.experimental import pallas as pl
from jax.experimental.pallas import tpu as pltpu
from jax.sharding import PartitionSpec as P

BF = jnp.bfloat16
GROUP = 4
MESH = pl.DeviceIdType.MESH
XS, YC, ZH = 4, 8, 4
TYS, TXS = 8, 32
AROUND = [(dr, dc) for dr in (-1, 0, 1) for dc in (-1, 0, 1) if (dr, dc) != (0, 0)]
E_ORDER = (4, 3, 5, 2, 6, 1, 7, 0)
DX_ORDER = (2, 1, 3, 0)
TY_ORDER = [(dx, dz) for dx in DX_ORDER for dz in (1, 0)]


def tables():
    alpha = 2 * np.pi * (np.arange(96) + 0.5) / 192
    beta = 2 * np.pi * (np.arange(128) + 0.5) / 256
    scale = 2.0 / (192 * 256)

    def split(a):
        hi = a.astype(ml_dtypes.bfloat16)
        return hi, (a - hi.astype(np.float64)).astype(ml_dtypes.bfloat16)

    def left(a):
        hi, lo = split(a)
        return np.concatenate([hi, lo, hi], axis=1)

    def right(a):
        hi, lo = split(a)
        return np.concatenate([hi, lo, hi], axis=0)

    def down(n):
        ang = np.outer(alpha, np.arange(n))
        return np.concatenate([np.cos(ang), np.sin(ang)], axis=0)

    def across(pos):
        ang = np.outer(pos, beta)
        return np.concatenate([np.cos(ang), np.sin(ang)], axis=1)

    patch = np.concatenate([np.arange(64), np.arange(192, 256), np.arange(64, 192)])
    return dict(
        ky=np.concatenate(split(down(128)), axis=1),
        kx=right(across(np.arange(128))),
        fy=left(down(64).T),
        fx=np.concatenate(split(across(np.arange(128)).T * scale), axis=1),
        qy=left(down(64)),
        ex=right(across(patch)),
        ey=left(down(192)),
        gy=left(down(192).T),
        gx=right(across(patch).T * scale),
    )

NAMES = ("ky", "kx", "fy", "fx", "qy", "ex", "ey", "gy", "gx")

def hilo(a):
    hi = a.astype(BF)
    return hi, (a - hi.astype(jnp.float32)).astype(BF)

def dot(a, b):
    return jnp.dot(a, b, preferred_element_type=jnp.float32)

def rows3(a):
    hi, lo = hilo(a)
    return jnp.concatenate([hi, hi, lo], axis=0)

def cols3(a):
    hi, lo = hilo(a)
    return jnp.concatenate([hi, hi, lo], axis=1)

def pairs(z):
    cc, cs, sc, ss = z[:96, :128], z[:96, 128:], z[96:, :128], z[96:, 128:]
    re = jnp.concatenate([cc - ss, cc + ss], axis=1)
    im = jnp.concatenate([sc + cs, sc - cs], axis=1)
    return re, im

def unpair(re, im):
    p, r, q, s = re[:, :128], re[:, 128:], im[:, :128], im[:, 128:]
    top = jnp.concatenate([p + r, s - q], axis=1)
    low = jnp.concatenate([-(q + s), r - p], axis=1)
    return jnp.concatenate([top, low], axis=0)

def mask_spectrum(patch, t, e2):
    packed = dot(cols3(patch), t["ex"][...])
    re, im = pairs(dot(t["ey"][...], rows3(packed)))
    e2[:96] = re
    e2[96:] = -im

def kernel_spectra(taps, t, k2, ps):
    wide = jnp.concatenate([c for pair in taps for c in pair], axis=1)
    half = dot(t["ky"][...], jnp.concatenate([wide, wide], axis=0))
    n = 2 * len(ps)
    tall = jnp.concatenate([half[:, 128 * i:128 * i + 128] for i in range(n)], axis=0)
    z = dot(cols3(tall), t["kx"][...])
    for i in range(n):
        re, im = pairs(z[192 * i:192 * i + 192])
        k2[ps[i // 2], i % 2, :96] = re
        k2[ps[i // 2], i % 2, 96:] = im


def fields_of(t, e2, k2, f, ps):
    er, ei = e2[:96], e2[96:]
    n = 2 * len(ps)
    parts = []
    for i in range(n):
        kr, ki = k2[ps[i // 2], i % 2, :96], k2[ps[i // 2], i % 2, 96:]
        parts.append(rows3(unpair(er * kr - ei * ki, er * ki + ei * kr)))
    y = dot(t["fy"][...], jnp.concatenate(parts, axis=1))
    hi, lo = hilo(jnp.concatenate([y[:, 256 * i:256 * i + 256] for i in range(n)], axis=0))
    first = dot(hi, t["fx"][...])
    res = first[:, :128] + first[:, 128:] + dot(lo, t["fx"][:, :128])
    for i, p in enumerate(ps):
        f[p] = res[128 * i:128 * i + 128]
    return [res[128 * i:128 * i + 128] for i in range(len(ps))]


def spread(t, k2, qs, ps, tot):
    packed = dot(cols3(jnp.concatenate(qs, axis=0)), t["kx"][...])
    for i in range(2 * len(ps)):
        qr, qi = pairs(dot(t["qy"][...], rows3(packed[64 * i:64 * i + 64])))
        kr, ki = k2[ps[i // 2], i % 2, :96], k2[ps[i // 2], i % 2, 96:]
        tot[:96] += qr * kr - qi * ki
        tot[96:] -= qi * kr + qr * ki


def back(t, tot):
    y = dot(t["gy"][...], rows3(unpair(tot[:96], tot[96:])))
    return dot(cols3(y), t["gx"][...])

def pack(a):
    low = lax.broadcasted_iota(jnp.int32, (32, 128), 1) < 64
    top, bot = a[:32], a[32:]
    return jnp.where(low, top, pltpu.roll(bot, 64, 1)), jnp.where(low, pltpu.roll(top, 64, 1), bot)

def unpack(a, b):
    low = lax.broadcasted_iota(jnp.int32, (32, 128), 1) < 64
    return jnp.concatenate([jnp.where(low, a, pltpu.roll(b, 64, 1)), jnp.where(low, pltpu.roll(a, 64, 1), b)], axis=0)

def kernel(*refs):
    (mask_in, target_in, sets, wts, zones, counts, zone_to_set) = refs[:7]
    hbm = dict(zip(NAMES, refs[7:7 + len(NAMES)]))
    n = 7 + len(NAMES)
    out = refs[n]
    t = dict(zip(NAMES, refs[n + 1:n + 1 + len(NAMES)]))
    (mask, target, value, halves, tall, side, chunks, column, info, sel, taps, wall, sv, wv, e2, k2, f, tot, co,
     gfull, ghalf, gtall, gside, want,
     tab_sem, in_sem, own_sem, s_info, r_info, s_info2, r_info2, s_w, r_w, s_w2, r_w2,
     s1, r1, s2, r2, s_m, r_m, s_m2, r_m2, s_g, r_g, s_g2, r_g2) = refs[n + 1 + len(NAMES):]

    ty, tx = lax.axis_index("ty"), lax.axis_index("tx")
    x, zl = ty // 2, ty % 2
    zh, yc = tx // YC, tx % YC
    me = ty * YC + yc

    def remote(src, dst, send, recv, to):
        return pltpu.make_async_remote_copy(src, dst, send, recv, device_id=to, device_id_type=MESH)

    def done(ref, sem):
        pltpu.make_async_copy(ref, ref, sem).wait()

    yc_line = [(yc + e) % YC for e in E_ORDER[:-1]]
    ty_line = [((x + dx) % XS) * 2 + (zl + dz) % 2 for dx, dz in TY_ORDER[:-1]]
    up = 2 * zl + ZH - 1

    def z_target(m):
        if m == 3:
            return x * 2 + (1 - zl), (zh + 2) % ZH
        return x * 2 + (m - 1), (zh + up) % ZH

    z_sources = [(x * 2 + 1, (zh + ZH - 1) % ZH), (x * 2, (zh + 1) % ZH), (x * 2 + (1 - zl), (zh + 2) % ZH)]
    def beside(dr, dc):
        return (ty + dr + TYS) % TYS, (tx + dc + TXS) % TXS

    bar = pltpu.get_barrier_semaphore()
    greet = [(a, b * YC + (yc + e) % YC) for a, b in z_sources for e in E_ORDER]
    greet += [(a, tx) for a in ty_line]
    greet += [(ty, zh * YC + b) for b in yc_line]
    greet += [beside(dr, dc) for dr, dc in AROUND if dc != 0]
    for to in greet:
        pl.semaphore_signal(bar, 1, device_id=to, device_id_type=MESH)

    copies_in = [pltpu.make_async_copy(mask_in, mask, in_sem.at[0]),
                 pltpu.make_async_copy(target_in, target, in_sem.at[1])]
    for c in copies_in:
        c.start()
    own = pltpu.make_async_copy(sets.at[me], chunks.at[tx], own_sem.at[0])
    own.start()
    tabs = [pltpu.make_async_copy(hbm[n], t[n], tab_sem.at[i]) for i, n in enumerate(NAMES)]
    for c in tabs:
        c.start()

    lane = lax.broadcasted_iota(jnp.int32, (1, 128), 1)
    my0, my1 = zone_to_set[zones[0]], zone_to_set[zones[1]]
    count = counts[0]
    sv[...] = jnp.where(lane % 2 == 0, my0, my1)
    wv[...] = jnp.concatenate([wts[...].astype(jnp.float32), jnp.zeros((1, 120), jnp.float32)], axis=1)
    for c in copies_in:
        c.wait()
    value[...] = 1.0 / (1.0 + jnp.exp(-mask[...]))
    halves[0], halves[1] = pack(value[...])

    pl.semaphore_wait(bar, len(greet))

    for a in ty_line:
        remote(sv, column.at[ty], s_info, r_info, (a, tx)).start()
    for m in (3, 2, 1):
        a, b = z_target(m)
        remote(wv, wall.at[yc, zh], s_w, r_w, (a, b * YC + yc)).start()
    for m in (3, 2, 1):
        a, b = z_target(m)
        for e in E_ORDER:
            y2 = (yc + e) % YC
            remote(sets.at[a * YC + y2], chunks.at[tx], s1, r1, (a, b * YC + y2)).start()
    for b in yc_line:
        remote(sets.at[ty * YC + b], chunks.at[tx], s1, r1, (ty, zh * YC + b)).start()
    column[ty] = sv[...]
    wall[yc, zh] = wv[...]
    done(column.at[pl.ds(0, 7)], r_info)
    merged = column[0]
    for i in range(1, TYS):
        merged = jnp.where(lane // 2 == i, column[i], merged)
    info[yc] = merged
    for b in yc_line:
        remote(info.at[yc], info.at[yc], s_info2, r_info2, (ty, zh * YC + b)).start()
    done(wall.at[0, pl.ds(0, 3)], r_w)
    for b in yc_line:
        remote(wall.at[yc], wall.at[yc], s_w2, r_w2, (ty, zh * YC + b)).start()
    for dr in (-1, 0, 1):
        for dc in (-1, 1):
            remote(halves.at[(dc + 1) // 2], side.at[(1 - dr) * 2 + (1 - dc) // 2], s_m, r_m, beside(dr, dc)).start()
    for dr in (-1, 1):
        remote(value, tall.at[(1 - dr) // 2], s_m2, r_m2, beside(dr, 0)).start()
    own.wait()
    done(info.at[pl.ds(0, 7)], r_info2)
    to_scalars = pltpu.make_async_copy(info, want, own_sem.at[0])
    to_scalars.start()
    to_scalars.wait()
    done(chunks.at[pl.ds(0, 31)], r1)


    def send_slot(j):
        for n, (dx, dz) in enumerate(TY_ORDER):
            ty2 = ((x + dx) % XS) * 2 + (zl + dz) % 2
            for e in E_ORDER:
                if (dx, dz, e) == (0, 0, 0):
                    continue
                y2 = (yc + e) % YC
                i = n * YC + e
                sel[j, i] = chunks[want[y2, 0, 2 * ty2 + j]]
                remote(sel.at[j, i], taps.at[j, me], s2.at[j], r2.at[j], (ty2, zh * YC + y2)).start()
        sel[j, 56] = chunks[(my0, my1)[j]]
        pltpu.make_async_copy(sel.at[j, 56], taps.at[j, me], r2.at[j]).start()

    send_slot(0)
    send_slot(1)

    for c in tabs:
        c.wait()
    done(side, r_m)
    done(tall, r_m2)

    def inside(dr, dc):
        row, col = ty + dr, tx + dc
        return (row >= 0) & (row < TYS) & (col >= 0) & (col < TXS)

    def gather(sides, talls, own_rows):
        blocks = []
        for dr in (-1, 0, 1):
            a, b = [jnp.where(inside(dr, dc), sides[(dr + 1) * 2 + (dc + 1) // 2], 0.0) for dc in (-1, 1)]
            mid = own_rows if dr == 0 else jnp.where(inside(dr, 0), talls[(dr + 1) // 2], 0.0)
            blocks.append((unpack(a, b), mid))
        return blocks

    blocks = gather(side, tall, value[...])
    mask_spectrum(jnp.concatenate([jnp.concatenate(b, axis=1) for b in blocks], axis=0), t, e2)
    done(column.at[pl.ds(0, 7)], s_info)
    done(wall.at[0, pl.ds(0, 3)], s_w)
    done(wall.at[pl.ds(0, 7)], r_w2)
    done(wall.at[pl.ds(0, 7)], s_w2)
    done(info.at[pl.ds(0, 7)], s_info2)
    done(side, s_m)
    done(tall, s_m2)
    done(chunks.at[pl.ds(0, 31)], s1)

    inverse = 1.0 / count.astype(jnp.float32)
    for j, s in enumerate((my0, my1)):
        row = wall[s % YC, s // YC]
        row = row * jnp.where(j < count, inverse, 0.0)
        for k in range(8):
            co[j * 8 + k] = jnp.broadcast_to(row[:, k:k + 1], (64, 128))

    aerial = jnp.zeros((64, 128), jnp.float32)
    for j in range(2):
        done(taps.at[j], r2.at[j])

        for h in range(0, 8, GROUP):
            chosen = [
                tuple(taps[j, 8 * k + 4 * i:8 * k + 4 * i + 4].reshape(128, 128) for i in range(2))
                for k in range(h, h + GROUP)
            ]
            kernel_spectra(chosen, t, k2, range(j * 8 + h, j * 8 + h + GROUP))
        for h in range(0, 8, GROUP):
            ps = range(j * 8 + h, j * 8 + h + GROUP)
            for p, fp in zip(ps, fields_of(t, e2, k2, f, ps)):
                aerial = aerial + co[p] * (fp[:64] * fp[:64] + fp[64:] * fp[64:])

    resist = 1.0 / (1.0 + jnp.exp(-8.0 * (aerial - 1.0)))
    out[0] = resist
    slope = 2.0 * (16.0 * (resist - target[...]) * 8.0 * resist * (1.0 - resist))
    tot[...] = jnp.zeros(tot.shape, jnp.float32)

    def some(h, carry):
        ps = [GROUP * h + i for i in range(GROUP)]
        spread(t, k2, [jnp.concatenate([slope * co[p]] * 2, axis=0) * f[p] for p in ps], ps, tot)
        return carry

    lax.fori_loop(0, 16 // GROUP, some, 0, unroll=2)
    g = back(t, tot)
    for dr in (-1, 1, 0):
        i = (dr + 1) * 2
        ghalf[i], ghalf[i + 1] = pack(g[(dr + 1) * 64:(dr + 2) * 64, :128])
        for dc in (-1, 1):
            remote(ghalf.at[i + (dc + 1) // 2], gside.at[(1 - dr) * 2 + (1 - dc) // 2], s_g, r_g, beside(dr, dc)).start()
        if dr != 0:
            gfull[(dr + 1) // 2] = g[(dr + 1) * 64:(dr + 2) * 64, 128:]
            remote(gfull.at[(dr + 1) // 2], gtall.at[(1 - dr) // 2], s_g2, r_g2, beside(dr, 0)).start()
    done(gtall, r_g2)
    done(gside, r_g)
    total = g[64:128, 128:]
    for from_sides, mid in gather(gside, gtall, 0.0):
        total = total + from_sides + mid
    m = value[...]
    out[1] = total * m * (1.0 - m)
    done(sel.at[0, pl.ds(0, 63)], s2.at[0])
    done(sel.at[1, pl.ds(0, 63)], s2.at[1])
    done(gtall, s_g2)
    done(gside, s_g)


def body(mask_param, target, kernel_sets, kernel_weights, tile_zones, tile_counts, zone_to_set):
    tb = tables()
    f32, i32, dma = jnp.float32, jnp.int32, pltpu.SemaphoreType.DMA
    any_, vmem = pl.BlockSpec(memory_space=pltpu.HBM), pl.BlockSpec(memory_space=pltpu.VMEM)
    smem = pl.BlockSpec(memory_space=pltpu.SMEM)
    scratch = [pltpu.VMEM(tb[n].shape, BF) for n in NAMES]
    scratch += [
        pltpu.VMEM((64, 128), f32), pltpu.VMEM((64, 128), f32), pltpu.VMEM((64, 128), f32),
        pltpu.VMEM((2, 32, 128), f32), pltpu.VMEM((2, 64, 128), f32), pltpu.VMEM((6, 32, 128), f32),
        pltpu.VMEM((32, 32, 128), BF), pltpu.VMEM((TYS, 1, 128), i32), pltpu.VMEM((YC, 1, 128), i32),
        pltpu.VMEM((2, 64, 32, 128), BF), pltpu.VMEM((2, 64, 32, 128), BF),
        pltpu.VMEM((YC, ZH, 1, 128), f32), pltpu.VMEM((1, 128), i32), pltpu.VMEM((1, 128), f32),
        pltpu.VMEM((192, 256), f32), pltpu.VMEM((16, 2, 192, 256), f32), pltpu.VMEM((16, 128, 128), f32),
        pltpu.VMEM((192, 256), f32), pltpu.VMEM((16, 64, 128), f32),
        pltpu.VMEM((2, 64, 128), f32), pltpu.VMEM((6, 32, 128), f32),
        pltpu.VMEM((2, 64, 128), f32), pltpu.VMEM((6, 32, 128), f32),
        pltpu.SMEM((YC, 1, 128), i32),
        dma((len(NAMES),)), dma((2,)), dma((1,)),
        dma, dma, dma, dma, dma, dma, dma, dma,
        dma, dma, dma((2,)), dma((2,)), dma, dma, dma, dma, dma, dma, dma, dma,
    ]
    out = pl.pallas_call(
        kernel,
        out_shape=jax.ShapeDtypeStruct((2, 64, 128), f32),
        in_specs=[any_, any_, any_, vmem, smem, smem, smem] + [any_] * len(NAMES),
        out_specs=vmem,
        scratch_shapes=scratch,
        compiler_params=pltpu.CompilerParams(
            collective_id=1, has_side_effects=True, vmem_limit_bytes=63 << 20
        ),
        name="litho",
    )(
        mask_param, target, kernel_sets.reshape(64, 32, 128), kernel_weights,
        tile_zones.reshape(2), tile_counts.reshape(1), zone_to_set,
        *[jnp.asarray(tb[n]) for n in NAMES],
    )
    return out[0], out[1]


def solution(mesh):
    in_specs = (
        P("ty", "tx"), P("ty", "tx"), P("tx", None, None, None, None), P("tx", None),
        P("ty", "tx", None), P("ty", "tx"), P(),
    )
    return jax.shard_map(
        body, mesh=mesh, in_specs=in_specs, out_specs=(P("ty", "tx"), P("ty", "tx")), check_vma=False
    )
```

```python
import functools

import jax
import jax.numpy as jnp
import ml_dtypes
import numpy as np
from jax import lax
from jax.experimental import pallas as pl
from jax.experimental.pallas import tpu as pltpu
from jax.sharding import PartitionSpec as P

BF = jnp.bfloat16
GROUP = 4
MESH = pl.DeviceIdType.MESH
XS, YC, ZH = 4, 8, 4
TYS, TXS = 8, 32
AROUND = [(dr, dc) for dr in (-1, 0, 1) for dc in (-1, 0, 1) if (dr, dc) != (0, 0)]
E_ORDER = (4, 3, 5, 2, 6, 1, 7, 0)
DX_ORDER = (2, 1, 3, 0)
TY_ORDER = [(dx, dz) for dx in DX_ORDER for dz in (1, 0)]


def tables():
    alpha = 2 * np.pi * (np.arange(96) + 0.5) / 192
    beta = 2 * np.pi * (np.arange(128) + 0.5) / 256
    scale = 2.0 / (192 * 256)

    def split(a):
        hi = a.astype(ml_dtypes.bfloat16)
        return hi, (a - hi.astype(np.float64)).astype(ml_dtypes.bfloat16)

    def left(a):
        hi, lo = split(a)
        return np.concatenate([hi, lo, hi], axis=1)

    def right(a):
        hi, lo = split(a)
        return np.concatenate([hi, lo, hi], axis=0)

    def down(n):
        ang = np.outer(alpha, np.arange(n))
        return np.concatenate([np.cos(ang), np.sin(ang)], axis=0)

    def across(pos):
        ang = np.outer(pos, beta)
        return np.concatenate([np.cos(ang), np.sin(ang)], axis=1)

    patch = np.concatenate([np.arange(64), np.arange(192, 256), np.arange(64, 192)])
    return dict(
        ky=np.concatenate(split(down(128)), axis=1),
        kx=right(across(np.arange(128))),
        fy=left(down(64).T),
        fx=np.concatenate(split(across(np.arange(128)).T * scale), axis=1),
        qy=left(down(64)),
        ex=right(across(patch)),
        ey=left(down(192)),
        gy=left(down(192).T[np.concatenate([np.arange(64), np.arange(128, 192), np.arange(64, 128)])]),
        gx=right(across(patch).T * scale),
    )

NAMES = ("ky", "kx", "fy", "fx", "qy", "ex", "ey", "gy", "gx")

def hilo(a):
    hi = a.astype(BF)
    return hi, (a - hi.astype(jnp.float32)).astype(BF)

def dot(a, b):
    return jnp.dot(a, b, preferred_element_type=jnp.float32)

def rows3(a):
    hi, lo = hilo(a)
    return jnp.concatenate([hi, hi, lo], axis=0)

def cols3(a):
    hi, lo = hilo(a)
    return jnp.concatenate([hi, hi, lo], axis=1)

def pairs(z):
    cc, cs, sc, ss = z[:96, :128], z[:96, 128:], z[96:, :128], z[96:, 128:]
    re = jnp.concatenate([cc - ss, cc + ss], axis=1)
    im = jnp.concatenate([sc + cs, sc - cs], axis=1)
    return re, im

def unpair(re, im):
    p, r, q, s = re[:, :128], re[:, 128:], im[:, :128], im[:, 128:]
    top = jnp.concatenate([p + r, s - q], axis=1)
    low = jnp.concatenate([-(q + s), r - p], axis=1)
    return jnp.concatenate([top, low], axis=0)

def mask_spectrum(patch, t, e2):
    packed = dot(cols3(patch), t["ex"][...])
    re, im = pairs(dot(t["ey"][...], rows3(packed)))
    e2[:96] = re
    e2[96:] = -im

def kernel_spectra(taps, t, k2, ps):
    wide = jnp.concatenate([c for pair in taps for c in pair], axis=1)
    half = dot(t["ky"][...], jnp.concatenate([wide, wide], axis=0))
    n = 2 * len(ps)
    tall = jnp.concatenate([half[:, 128 * i:128 * i + 128] for i in range(n)], axis=0)
    z = dot(cols3(tall), t["kx"][...])
    for i in range(n):
        re, im = pairs(z[192 * i:192 * i + 192])
        k2[ps[i // 2], i % 2, :96] = re
        k2[ps[i // 2], i % 2, 96:] = im


def fields_of(t, e2, k2, f, ps):
    er, ei = e2[:96], e2[96:]
    n = 2 * len(ps)
    parts = []
    for i in range(n):
        kr, ki = k2[ps[i // 2], i % 2, :96], k2[ps[i // 2], i % 2, 96:]
        parts.append(rows3(unpair(er * kr - ei * ki, er * ki + ei * kr)))
    y = dot(t["fy"][...], jnp.concatenate(parts, axis=1))
    hi, lo = hilo(jnp.concatenate([y[:, 256 * i:256 * i + 256] for i in range(n)], axis=0))
    first = dot(hi, t["fx"][...])
    res = first[:, :128] + first[:, 128:] + dot(lo, t["fx"][:, :128])
    for i, p in enumerate(ps):
        f[p] = res[128 * i:128 * i + 128]
    return [res[128 * i:128 * i + 128] for i in range(len(ps))]


def spread(t, k2, qs, ps, tot):
    packed = dot(cols3(jnp.concatenate(qs, axis=0)), t["kx"][...])
    for i in range(2 * len(ps)):
        qr, qi = pairs(dot(t["qy"][...], rows3(packed[64 * i:64 * i + 64])))
        kr, ki = k2[ps[i // 2], i % 2, :96], k2[ps[i // 2], i % 2, 96:]
        tot[:96] += qr * kr - qi * ki
        tot[96:] -= qi * kr + qr * ki


def back(t, tot):
    tall = rows3(unpair(tot[:96], tot[96:]))
    return [dot(cols3(dot(t["gy"][a:b, :], tall)), t["gx"][...]) for a, b in ((0, 128), (128, 192))]


def pack(a):
    low = lax.broadcasted_iota(jnp.int32, (32, 128), 1) < 64
    top, bot = a[:32], a[32:]
    return jnp.where(low, top, pltpu.roll(bot, 64, 1)), jnp.where(low, pltpu.roll(top, 64, 1), bot)

def unpack(a, b):
    low = lax.broadcasted_iota(jnp.int32, (32, 128), 1) < 64
    return jnp.concatenate([jnp.where(low, a, pltpu.roll(b, 64, 1)), jnp.where(low, pltpu.roll(a, 64, 1), b)], axis=0)

def kernel(*refs):
    (mask_in, target_in, sets, wts, zones, counts, zone_to_set) = refs[:7]
    hbm = dict(zip(NAMES, refs[7:7 + len(NAMES)]))
    n = 7 + len(NAMES)
    out = refs[n]
    t = dict(zip(NAMES, refs[n + 1:n + 1 + len(NAMES)]))
    (mask, target, value, halves, tall, side, chunks, column, info, sel, taps, wall, sv, wv, e2, k2, f, tot, co,
     gfull, ghalf, gtall, gside, want,
     tab_sem, in_sem, own_sem, s_info, r_info, s_info2, r_info2, s_w, r_w, s_w2, r_w2,
     s1, r1, s2, r2, s_m, r_m, s_m2, r_m2, s_g, r_g, s_g2, r_g2) = refs[n + 1 + len(NAMES):]

    ty, tx = lax.axis_index("ty"), lax.axis_index("tx")
    x, zl = ty // 2, ty % 2
    zh, yc = tx // YC, tx % YC
    me = ty * YC + yc

    def remote(src, dst, send, recv, to):
        return pltpu.make_async_remote_copy(src, dst, send, recv, device_id=to, device_id_type=MESH)

    def done(ref, sem):
        pltpu.make_async_copy(ref, ref, sem).wait()

    yc_line = [(yc + e) % YC for e in E_ORDER[:-1]]
    ty_line = [((x + dx) % XS) * 2 + (zl + dz) % 2 for dx, dz in TY_ORDER[:-1]]
    up = 2 * zl + ZH - 1

    def z_target(m):
        if m == 3:
            return x * 2 + (1 - zl), (zh + 2) % ZH
        return x * 2 + (m - 1), (zh + up) % ZH

    z_sources = [(x * 2 + 1, (zh + ZH - 1) % ZH), (x * 2, (zh + 1) % ZH), (x * 2 + (1 - zl), (zh + 2) % ZH)]
    def beside(dr, dc):
        return (ty + dr + TYS) % TYS, (tx + dc + TXS) % TXS

    bar = pltpu.get_barrier_semaphore()
    greet = [(a, b * YC + (yc + e) % YC) for a, b in z_sources for e in E_ORDER]
    greet += [(a, tx) for a in ty_line]
    greet += [(ty, zh * YC + b) for b in yc_line]
    greet += [beside(dr, dc) for dr, dc in AROUND if dc != 0]
    for to in greet:
        pl.semaphore_signal(bar, 1, device_id=to, device_id_type=MESH)

    copies_in = [pltpu.make_async_copy(mask_in, mask, in_sem.at[0]),
                 pltpu.make_async_copy(target_in, target, in_sem.at[1])]
    for c in copies_in:
        c.start()
    own = pltpu.make_async_copy(sets.at[me], chunks.at[tx], own_sem.at[0])
    own.start()
    tabs = [pltpu.make_async_copy(hbm[n], t[n], tab_sem.at[i]) for i, n in enumerate(NAMES)]
    for c in tabs:
        c.start()

    lane = lax.broadcasted_iota(jnp.int32, (1, 128), 1)
    my0, my1 = zone_to_set[zones[0]], zone_to_set[zones[1]]
    count = counts[0]
    sv[...] = jnp.where(lane % 2 == 0, my0, my1)
    wv[...] = jnp.concatenate([wts[...].astype(jnp.float32), jnp.zeros((1, 120), jnp.float32)], axis=1)
    for c in copies_in:
        c.wait()
    value[...] = 1.0 / (1.0 + jnp.exp(-mask[...]))
    halves[0], halves[1] = pack(value[...])

    pl.semaphore_wait(bar, len(greet))

    for a in ty_line:
        remote(sv, column.at[ty], s_info, r_info, (a, tx)).start()
    for m in (3, 2, 1):
        a, b = z_target(m)
        remote(wv, wall.at[yc, zh], s_w, r_w, (a, b * YC + yc)).start()
    for m in (3, 2, 1):
        a, b = z_target(m)
        for e in E_ORDER:
            y2 = (yc + e) % YC
            remote(sets.at[a * YC + y2], chunks.at[tx], s1, r1, (a, b * YC + y2)).start()
    for b in yc_line:
        remote(sets.at[ty * YC + b], chunks.at[tx], s1, r1, (ty, zh * YC + b)).start()
    column[ty] = sv[...]
    wall[yc, zh] = wv[...]
    done(column.at[pl.ds(0, 7)], r_info)
    merged = column[0]
    for i in range(1, TYS):
        merged = jnp.where(lane // 2 == i, column[i], merged)
    info[yc] = merged
    for b in yc_line:
        remote(info.at[yc], info.at[yc], s_info2, r_info2, (ty, zh * YC + b)).start()
    done(wall.at[0, pl.ds(0, 3)], r_w)
    for b in yc_line:
        remote(wall.at[yc], wall.at[yc], s_w2, r_w2, (ty, zh * YC + b)).start()
    for dr in (-1, 0, 1):
        for dc in (-1, 1):
            remote(halves.at[(dc + 1) // 2], side.at[(1 - dr) * 2 + (1 - dc) // 2], s_m, r_m, beside(dr, dc)).start()
    for dr in (-1, 1):
        remote(value, tall.at[(1 - dr) // 2], s_m2, r_m2, beside(dr, 0)).start()
    own.wait()
    done(info.at[pl.ds(0, 7)], r_info2)
    to_scalars = pltpu.make_async_copy(info, want, own_sem.at[0])
    to_scalars.start()
    to_scalars.wait()
    done(chunks.at[pl.ds(0, 31)], r1)


    def send_slot(j):
        for n, (dx, dz) in enumerate(TY_ORDER):
            ty2 = ((x + dx) % XS) * 2 + (zl + dz) % 2
            for e in E_ORDER:
                if (dx, dz, e) == (0, 0, 0):
                    continue
                y2 = (yc + e) % YC
                i = n * YC + e
                sel[j, i] = chunks[want[y2, 0, 2 * ty2 + j]]
                remote(sel.at[j, i], taps.at[j, me], s2.at[j], r2.at[j], (ty2, zh * YC + y2)).start()
        sel[j, 56] = chunks[(my0, my1)[j]]
        pltpu.make_async_copy(sel.at[j, 56], taps.at[j, me], r2.at[j]).start()

    send_slot(0)
    send_slot(1)

    for c in tabs:
        c.wait()
    done(side, r_m)
    done(tall, r_m2)

    def inside(dr, dc):
        row, col = ty + dr, tx + dc
        return (row >= 0) & (row < TYS) & (col >= 0) & (col < TXS)

    def gather(sides, talls, own_rows):
        blocks = []
        for dr in (-1, 0, 1):
            a, b = [jnp.where(inside(dr, dc), sides[(dr + 1) * 2 + (dc + 1) // 2], 0.0) for dc in (-1, 1)]
            mid = own_rows if dr == 0 else jnp.where(inside(dr, 0), talls[(dr + 1) // 2], 0.0)
            blocks.append((unpack(a, b), mid))
        return blocks

    blocks = gather(side, tall, value[...])
    mask_spectrum(jnp.concatenate([jnp.concatenate(b, axis=1) for b in blocks], axis=0), t, e2)
    done(column.at[pl.ds(0, 7)], s_info)
    done(wall.at[0, pl.ds(0, 3)], s_w)
    done(wall.at[pl.ds(0, 7)], r_w2)
    done(wall.at[pl.ds(0, 7)], s_w2)
    done(info.at[pl.ds(0, 7)], s_info2)
    done(side, s_m)
    done(tall, s_m2)
    done(chunks.at[pl.ds(0, 31)], s1)

    inverse = 1.0 / count.astype(jnp.float32)
    for j, s in enumerate((my0, my1)):
        row = wall[s % YC, s // YC]
        row = row * jnp.where(j < count, inverse, 0.0)
        for k in range(8):
            co[j * 8 + k] = jnp.broadcast_to(row[:, k:k + 1], (64, 128))

    aerial = jnp.zeros((64, 128), jnp.float32)
    for j in range(2):
        done(taps.at[j], r2.at[j])

        for h in range(0, 8, GROUP):
            chosen = [
                tuple(taps[j, 8 * k + 4 * i:8 * k + 4 * i + 4].reshape(128, 128) for i in range(2))
                for k in range(h, h + GROUP)
            ]
            kernel_spectra(chosen, t, k2, range(j * 8 + h, j * 8 + h + GROUP))
        for h in range(0, 8, GROUP):
            ps = range(j * 8 + h, j * 8 + h + GROUP)
            for p, fp in zip(ps, fields_of(t, e2, k2, f, ps)):
                aerial = aerial + co[p] * (fp[:64] * fp[:64] + fp[64:] * fp[64:])

    resist = 1.0 / (1.0 + jnp.exp(-8.0 * (aerial - 1.0)))
    out[0] = resist
    slope = 2.0 * (16.0 * (resist - target[...]) * 8.0 * resist * (1.0 - resist))
    tot[...] = jnp.zeros(tot.shape, jnp.float32)

    def some(h, carry):
        ps = [GROUP * h + i for i in range(GROUP)]
        spread(t, k2, [jnp.concatenate([slope * co[p]] * 2, axis=0) * f[p] for p in ps], ps, tot)
        return carry

    lax.fori_loop(0, 16 // GROUP, some, 0, unroll=2)
    outer, middle = back(t, tot)
    for dr in (-1, 1, 0):
        i = (dr + 1) * 2
        g = middle if dr == 0 else outer[(dr + 1) * 32:(dr + 1) * 32 + 64]
        ghalf[i], ghalf[i + 1] = pack(g[:, :128])
        for dc in (-1, 1):
            remote(ghalf.at[i + (dc + 1) // 2], gside.at[(1 - dr) * 2 + (1 - dc) // 2], s_g, r_g, beside(dr, dc)).start()
        if dr != 0:
            gfull[(dr + 1) // 2] = g[:, 128:]
            remote(gfull.at[(dr + 1) // 2], gtall.at[(1 - dr) // 2], s_g2, r_g2, beside(dr, 0)).start()
    done(gtall, r_g2)
    done(gside, r_g)
    total = middle[:, 128:]
    for from_sides, mid in gather(gside, gtall, 0.0):
        total = total + from_sides + mid
    m = value[...]
    out[1] = total * m * (1.0 - m)
    done(sel.at[0, pl.ds(0, 63)], s2.at[0])
    done(sel.at[1, pl.ds(0, 63)], s2.at[1])
    done(gtall, s_g2)
    done(gside, s_g)


def body(mask_param, target, kernel_sets, kernel_weights, tile_zones, tile_counts, zone_to_set):
    tb = tables()
    f32, i32, dma = jnp.float32, jnp.int32, pltpu.SemaphoreType.DMA
    any_, vmem = pl.BlockSpec(memory_space=pltpu.HBM), pl.BlockSpec(memory_space=pltpu.VMEM)
    smem = pl.BlockSpec(memory_space=pltpu.SMEM)
    scratch = [pltpu.VMEM(tb[n].shape, BF) for n in NAMES]
    scratch += [
        pltpu.VMEM((64, 128), f32), pltpu.VMEM((64, 128), f32), pltpu.VMEM((64, 128), f32),
        pltpu.VMEM((2, 32, 128), f32), pltpu.VMEM((2, 64, 128), f32), pltpu.VMEM((6, 32, 128), f32),
        pltpu.VMEM((32, 32, 128), BF), pltpu.VMEM((TYS, 1, 128), i32), pltpu.VMEM((YC, 1, 128), i32),
        pltpu.VMEM((2, 64, 32, 128), BF), pltpu.VMEM((2, 64, 32, 128), BF),
        pltpu.VMEM((YC, ZH, 1, 128), f32), pltpu.VMEM((1, 128), i32), pltpu.VMEM((1, 128), f32),
        pltpu.VMEM((192, 256), f32), pltpu.VMEM((16, 2, 192, 256), f32), pltpu.VMEM((16, 128, 128), f32),
        pltpu.VMEM((192, 256), f32), pltpu.VMEM((16, 64, 128), f32),
        pltpu.VMEM((2, 64, 128), f32), pltpu.VMEM((6, 32, 128), f32),
        pltpu.VMEM((2, 64, 128), f32), pltpu.VMEM((6, 32, 128), f32),
        pltpu.SMEM((YC, 1, 128), i32),
        dma((len(NAMES),)), dma((2,)), dma((1,)),
        dma, dma, dma, dma, dma, dma, dma, dma,
        dma, dma, dma((2,)), dma((2,)), dma, dma, dma, dma, dma, dma, dma, dma,
    ]
    out = pl.pallas_call(
        kernel,
        out_shape=jax.ShapeDtypeStruct((2, 64, 128), f32),
        in_specs=[any_, any_, any_, vmem, smem, smem, smem] + [any_] * len(NAMES),
        out_specs=vmem,
        scratch_shapes=scratch,
        compiler_params=pltpu.CompilerParams(
            collective_id=1, has_side_effects=True, vmem_limit_bytes=63 << 20
        ),
        name="litho",
    )(
        mask_param, target, kernel_sets.reshape(64, 32, 128), kernel_weights,
        tile_zones.reshape(2), tile_counts.reshape(1), zone_to_set,
        *[jnp.asarray(tb[n]) for n in NAMES],
    )
    return out[0], out[1]


def solution(mesh):
    in_specs = (
        P("ty", "tx"), P("ty", "tx"), P("tx", None, None, None, None), P("tx", None),
        P("ty", "tx", None), P("ty", "tx"), P(),
    )
    return jax.shard_map(
        body, mesh=mesh, in_specs=in_specs, out_specs=(P("ty", "tx"), P("ty", "tx")), check_vma=False
    )
```
